256 devices in a mesh: ex: 8 (over z), ey: 16 (over y, x), tp: 2 (over core).
Axes of the slice: x: 4, y: 4, z: 8, core: 2. Of those that a mesh axis runs over, the one named last changes fastest.
Arguments:
- layer_input: bfloat16 [8192, 4096], P(('ex', 'ey'), 'tp'), may hold values from -6 to 6
- out_grad: bfloat16 [8192, 4096], P(('ex', 'ey'), 'tp'), may hold values from -6 to 6
- gate_prob: bfloat16 [8192, 8], P(('ex', 'ey')), may hold values from 0.099609375 to 1
- expert_ids: int32 [8192, 8], P(('ex', 'ey')), may hold values from 0 to 127, all different within a row; in each aligned block of 64 rows (0 to 63, 64 to 127, ...) at most 6 rows name the same one
- gate_weight: bfloat16 [128, 4096, 768], P(('ex', 'ey'), None, 'tp'), may hold values from -0.09375 to 0.09375
- up_weight: bfloat16 [128, 4096, 768], P(('ex', 'ey'), None, 'tp'), may hold values from -0.09375 to 0.09375
- down_weight: bfloat16 [128, 768, 4096], P(('ex', 'ey'), 'tp'), may hold values from -0.21875 to 0.21875
Outputs:
- input_grad: bfloat16 [8192, 4096], P(('ex', 'ey'), 'tp')
- prob_grad: bfloat16 [8192, 8], P(('ex', 'ey'))
- down_grad: bfloat16 [128, 768, 4096], P(('ex', 'ey'), 'tp')
The draws below stay inside these ranges and needn't reach their ends.
Inputs may be any that keep to these rules, and one draw needn't show every extreme that they name: `expert_ids`: each row names 8 different experts. In each aligned block of 64 rows (the tokens of one index of ex and ey) no expert is named by more than 6 rows, a bound that some block reaches.
All inputs are finite; a program needn't handle non-finite values.
Results may differ from the reference program's by a relative error of at most 0.0065.
Values may be sent and summed in bfloat16 or wider, within the bound.
No kernel may reach another device: no remote copies, remote signals or barrier semaphores. Data moves between devices by JAX's collectives and lax.ppermute only.
A program may use at most 128 MiB of HBM per device.

```python
import math
import jax
import jax.numpy as jnp
import numpy as np
from jax import lax

D = 4096
TOPK = 8
HID = 768
TOK_DEV = 64
EXPERTS = 128
TOKENS = 8192
CAP = 6
SLOTS = 768
N_TP = 2


def levels(own_key, extent, split, smallest, top_value):
    def one(dim, shards_of):
        draws = jax.random.uniform(jax.random.fold_in(jax.random.fold_in(own_key, 6), dim), (shards_of,), jnp.float32, smallest / len(split), top_value / len(split))
        return jnp.repeat(jnp.exp(draws), extent[dim] // shards_of).reshape((-1,) + (1,) * (len(extent) - dim - 1))

    factor_of = one(*split[0])
    for cut in split[1:]:
        factor_of = factor_of * one(*cut)
    return factor_of


def deal_out(rng, own, number, rows, number_of, top, most, lean):
    order = jax.random.permutation(rng, number_of)
    packed, usual = portions_of(number_of, rows * top, most, lean, True), portions_of(number_of, rows * top, most, lean, False)
    places = jnp.arange(number_of)

    def named(sizes, offset_by):
        used = int((sizes > 0).sum())
        fixed = max(1, used // 4)
        moved = fixed + (places - fixed + offset_by * (used - fixed)) % max(1, number_of - fixed)
        return jnp.zeros((number_of,), jnp.int32).at[order[jnp.where(places < fixed, places, moved)]].set(jnp.asarray(sizes, jnp.int32))

    sizes = jnp.where(number % 4 == 0, named(packed, number // 4), named(usual, number - number // 4 - 1))
    mixed = jax.random.permutation(jax.random.fold_in(own, 3), number_of)
    giver, receiver = mixed[0:number_of // 2 * 2:2], mixed[1:number_of // 2 * 2:2]
    room = jnp.minimum(sizes[giver] - 1, most - sizes[receiver]) // 2
    room = jnp.where((giver == order[0]) | (receiver == order[0]) | (sizes[receiver] == 0), 0, jnp.maximum(room, 0))
    moved = jax.random.randint(jax.random.fold_in(own, 4), (number_of // 2,), 0, 1 << 20) % (room + 1)
    sizes = sizes.at[giver].add(-moved).at[receiver].add(moved)
    items = jnp.searchsorted(jnp.cumsum(sizes), jnp.arange(rows * top), side="right").astype(jnp.int32)
    listing = items.reshape(top, rows).T
    listing = listing[jax.random.permutation(jax.random.fold_in(own, 1), rows)]
    offset_by = jax.random.randint(jax.random.fold_in(own, 2), (rows, 1), 0, top)
    return jnp.take_along_axis(listing, (jnp.arange(top)[None, :] + offset_by) % top, axis=1)


def portions_of(number_of, total, reach, slope, full):
    portions = [(1 << 20) // math.isqrt(grade ** slope) + 1 for grade in range(1, number_of + 1)]
    largest = reach if full else min(reach, max(-(-total // number_of), total * portions[0] // sum(portions)))
    least = 1 if total - largest >= number_of - 1 else 0
    counts, spare = [largest] + [least] * (number_of - 1), total - largest - least * (number_of - 1)
    while spare > 0:
        free = [i for i in range(1, number_of) if counts[i] < largest] or [i for i in range(1, number_of) if counts[i] < reach]
        mass, budget = sum([portions[i] for i in free]), spare
        for i in free:
            more = min(reach - counts[i], max(1, budget * portions[i] // mass), spare)
            counts[i] = counts[i] + more
            spare = spare - more
    return np.array(counts)


def noise(stream_key, extent, spread, limit, shards=(), kind=jnp.bfloat16):
    values = spread * jax.random.normal(stream_key, extent, jnp.float32)
    if shards:
        values = values * levels(stream_key, extent, shards, -0.22, 0.18)
    return jnp.clip(values, -limit, limit).astype(kind)


def setup_inputs(seed: int = 0) -> dict:
    arg_keys = jax.random.split(jax.random.key(seed), 8)
    layer_input = noise(arg_keys[0], (TOKENS, D), 1.0, 6.0, ((0, 128), (1, 2)))
    out_grad = noise(arg_keys[1], (TOKENS, D), 1.0, 6.0, ((0, 128), (1, 2)))
    gate_prob = jnp.clip(jnp.exp(math.log(1.0) - 2.306499 * jax.random.uniform(arg_keys[2], (TOKENS, TOPK), jnp.float32) ** levels(arg_keys[2], (TOKENS, TOPK), ((0, 128),), -0.2, 0.2)), 0.099609375, 1.0).astype(jnp.bfloat16)
    expert_ids_keys = jax.random.split(jax.random.fold_in(arg_keys[3], 1), TOKENS // TOK_DEV)
    expert_ids_turns = jax.random.permutation(jax.random.fold_in(arg_keys[3], 3), TOKENS // TOK_DEV)
    expert_ids = jax.vmap(lambda own, number: deal_out(jax.random.fold_in(arg_keys[3], 2), own, number, TOK_DEV, EXPERTS, TOPK, CAP, 2))(expert_ids_keys, expert_ids_turns).reshape((TOKENS, TOPK))
    gate_weight = noise(arg_keys[4], (EXPERTS, D, HID), D ** -0.5, 0.09375, ((0, 128), (2, 2)))
    up_weight = noise(arg_keys[5], (EXPERTS, D, HID), D ** -0.5, 0.09375, ((0, 128), (2, 2)))
    down_weight = noise(arg_keys[6], (EXPERTS, HID, D), HID ** -0.5, 0.21875, ((0, 128), (1, 2)))
    return dict(layer_input=layer_input, out_grad=out_grad, gate_prob=gate_prob, expert_ids=expert_ids, gate_weight=gate_weight, up_weight=up_weight, down_weight=down_weight)


def rounded(values):
    return lax.optimization_barrier(values.astype(jnp.bfloat16)).astype(jnp.float32)


def reference(layer_input, out_grad, gate_prob, expert_ids, gate_weight, up_weight, down_weight):
    routes = TOKENS * TOPK
    group = HID // N_TP
    flat_ids = expert_ids.reshape(routes).astype(jnp.int32)
    onehot = (flat_ids[:, None] == jnp.arange(EXPERTS, dtype=jnp.int32)[None, :]).astype(jnp.int32)
    before = jnp.sum((jnp.cumsum(onehot, axis=0) - onehot) * onehot, axis=1).astype(jnp.int32)
    table = jnp.full((EXPERTS, SLOTS), routes, jnp.int32).at[flat_ids, before].set(jnp.arange(routes, dtype=jnp.int32))
    inputs_pad = jnp.concatenate([layer_input, jnp.zeros((1, D), layer_input.dtype)], axis=0)
    grads_pad = jnp.concatenate([out_grad, jnp.zeros((1, D), out_grad.dtype)], axis=0)
    probs_pad = jnp.concatenate([gate_prob.reshape(routes).astype(jnp.float32), jnp.zeros((1,), jnp.float32)], axis=0)

    def per_expert(carry, item):
        acc_rows, acc_probs = carry
        index, slot_rows = item
        token_idx = (slot_rows // TOPK).astype(jnp.int32)
        rows_in = inputs_pad[token_idx].astype(jnp.float32)
        rows_grad = grads_pad[token_idx].astype(jnp.float32)
        route_weight = probs_pad[slot_rows][:, None]
        gate_mat = gate_weight[index].astype(jnp.float32)
        up_mat = up_weight[index].astype(jnp.float32)
        down_mat = down_weight[index].astype(jnp.float32)
        gate_pre = jnp.dot(rows_in, gate_mat)
        up_pre = jnp.dot(rows_in, up_mat)
        gate_sigmoid = jax.nn.sigmoid(gate_pre)
        silu_gate = gate_pre * gate_sigmoid
        hidden_act = silu_gate * up_pre
        weighted = rounded(route_weight * hidden_act)
        down_part = jnp.dot(weighted.T, rows_grad).astype(jnp.bfloat16)
        hidden_grad = jnp.dot(rows_grad, down_mat.T)
        prob_part = jnp.sum(hidden_grad * hidden_act, axis=1)
        gate_grad = rounded(route_weight * hidden_grad * up_pre * gate_sigmoid * (1.0 + gate_pre * (1.0 - gate_sigmoid)))
        up_grad = rounded(route_weight * hidden_grad * silu_gate)
        parts = jnp.einsum("rjh,djh->jrd", gate_grad.reshape(-1, N_TP, group), gate_mat.reshape(D, N_TP, group))
        parts = parts + jnp.einsum("rjh,djh->jrd", up_grad.reshape(-1, N_TP, group), up_mat.reshape(D, N_TP, group))
        route_grad = rounded(jnp.sum(rounded(parts), axis=0))
        acc_rows = acc_rows.at[token_idx].add(route_grad)
        acc_probs = acc_probs.at[slot_rows].set(prob_part)
        return (acc_rows, acc_probs), down_part

    start = (jnp.zeros((TOKENS + 1, D), jnp.float32), jnp.zeros((routes + 1,), jnp.float32))
    (acc_rows, acc_probs), down_grad = lax.scan(per_expert, start, (jnp.arange(EXPERTS, dtype=jnp.int32), table))
    input_grad = acc_rows[:TOKENS].astype(jnp.bfloat16)
    prob_grad = acc_probs[:routes].reshape(TOKENS, TOPK).astype(jnp.bfloat16)
    return (input_grad, prob_grad, down_grad)
```

```python
import jax
import jax.numpy as jnp
from jax import lax
from jax.sharding import PartitionSpec as P

LANES = 128


def dot(a, b, dims=((1,), (0,))):
    return lax.dot_general(a, b, (dims, ((), ())), preferred_element_type=jnp.float32)


def body(layer_input, out_grad, gate_prob, expert_ids, gate_weight, up_weight, down_weight):
    bf16, f32 = jnp.bfloat16, jnp.float32
    tok_rows, choose = expert_ids.shape
    half = layer_input.shape[1]
    hid = gate_weight.shape[2]
    n_high, n_low = lax.axis_size("ex"), lax.axis_size("ey")
    experts = n_high * n_low
    capacity = 3 * tok_rows * choose // (2 * experts) * n_high
    tokens = tok_rows * n_high
    slots = n_low * capacity
    high, low, core = lax.axis_index("ex"), lax.axis_index("ey"), lax.axis_index("tp")
    swap = [(0, 1), (1, 0)]

    own = core * half
    other = half - own
    gate_w, up_w, down_w = gate_weight[0], up_weight[0], down_weight[0]

    def in_order(w, axis):
        return (
            lax.dynamic_slice_in_dim(w, own, half, axis),
            lax.dynamic_slice_in_dim(w, other, half, axis),
        )

    both = jnp.concatenate([gate_w, up_w], axis=1)
    both_own, both_other = in_order(both, 0)
    down_own, down_other = in_order(down_w, 1)

    meta = jnp.concatenate(
        [
            expert_ids.astype(bf16),
            gate_prob,
            jnp.zeros((tok_rows, LANES - 2 * choose), bf16),
        ],
        axis=1,
    )
    packed = lax.all_gather(
        jnp.concatenate([layer_input, meta], axis=1), "ex", axis=0, tiled=True
    )
    all_grads = lax.all_gather(out_grad, "ex", axis=0, tiled=True)
    all_inputs = packed[:, :half]
    all_ids = packed[:, half : half + choose].astype(jnp.int32).T
    all_probs = packed[:, half + choose : half + 2 * choose].astype(f32).T

    mine = lax.broadcasted_iota(jnp.int32, (n_low, 1, 1), 0) + high * n_low
    named = all_ids[None, :, :] == mine
    chosen = jnp.sum(named.astype(f32), axis=1)
    weight = jnp.sum(jnp.where(named, all_probs[None], 0.0), axis=1)
    earlier = (
        lax.broadcasted_iota(jnp.int32, (tokens, tokens), 0)
        < lax.broadcasted_iota(jnp.int32, (tokens, tokens), 1)
    ).astype(bf16)
    rank = dot(chosen.astype(bf16), earlier).astype(jnp.int32)
    rank = jnp.where(chosen > 0, rank, -1)
    hit = rank[:, None, :] == lax.broadcasted_iota(jnp.int32, (1, capacity, 1), 1)
    pick = hit.astype(bf16).reshape(slots, tokens)
    pick_weighted = jnp.where(hit, weight[:, None, :], 0.0).astype(bf16).reshape(slots, tokens)

    def across(x):
        return lax.all_to_all(x, "ey", split_axis=0, concat_axis=0, tiled=True)

    rows_own = across(dot(pick, all_inputs).astype(bf16))
    rows_other = lax.ppermute(rows_own, "tp", swap)
    grads_own = across(dot(pick_weighted, all_grads).astype(bf16))
    grads_other = lax.ppermute(grads_own, "tp", swap)

    pre = dot(rows_own, both_own) + dot(rows_other, both_other)
    gate_pre, up_pre = pre[:, :hid], pre[:, hid:]
    gate_sigmoid = jax.nn.sigmoid(gate_pre)
    silu_gate = gate_pre * gate_sigmoid
    hidden_act = silu_gate * up_pre
    act = hidden_act.astype(bf16)

    hidden_grad = dot(grads_own, down_own, ((1,), (1,))) + dot(
        grads_other, down_other, ((1,), (1,))
    )
    prob_part = jnp.sum(hidden_grad * hidden_act, axis=1, keepdims=True)
    prob_total = prob_part + lax.ppermute(prob_part, "tp", swap)
    gate_grad = hidden_grad * up_pre * gate_sigmoid * (1.0 + gate_pre * (1.0 - gate_sigmoid))
    up_grad = hidden_grad * silu_gate
    grad_both = jnp.concatenate([gate_grad.astype(bf16), up_grad.astype(bf16)], axis=1)

    part_other = dot(grad_both, both_other, ((1,), (1,))).astype(bf16)
    part_here = lax.ppermute(part_other, "tp", swap)
    part_own = dot(grad_both, both_own, ((1,), (1,)))
    back = (part_own + part_here.astype(f32)).astype(bf16)
    lane = lax.broadcasted_iota(jnp.int32, (1, LANES), 1)
    back_probs = jnp.where(lane == high * n_low + low, prob_total, 0.0).astype(bf16)
    home = across(jnp.concatenate([back, back_probs], axis=1))

    grad_here = dot(act, grads_own, ((0,), (0,))).astype(bf16)
    grad_there = dot(act, grads_other, ((0,), (0,))).astype(bf16)
    first = core == 0
    down_grad = jnp.concatenate(
        [jnp.where(first, grad_here, grad_there), jnp.where(first, grad_there, grad_here)],
        axis=1,
    )

    sums = dot(pick, home, ((0,), (0,))).astype(bf16)
    final = lax.psum_scatter(sums, "ex", scatter_dimension=0, tiled=True)
    input_grad = final[:, :half]
    by_expert = final[:, half:].astype(f32)
    found = jnp.sum(
        jnp.where(expert_ids[:, :, None] == lane[None], by_expert[:, None, :], 0.0), axis=2
    )
    prob_grad = (found / gate_prob.astype(f32)).astype(bf16)
    return (input_grad, prob_grad, down_grad[None])


def solution(mesh):
    return jax.shard_map(
        body,
        mesh=mesh,
        in_specs=(
            P(("ex", "ey"), "tp"),
            P(("ex", "ey"), "tp"),
            P(("ex", "ey"), None),
            P(("ex", "ey"), None),
            P(("ex", "ey"), None, "tp"),
            P(("ex", "ey"), None, "tp"),
            P(("ex", "ey"), "tp", None),
        ),
        out_specs=(P(("ex", "ey"), "tp"), P(("ex", "ey"), None), P(("ex", "ey"), "tp", None)),
        check_vma=False,
    )
```

```python
import jax
import jax.numpy as jnp
from jax import lax
from jax.experimental import pallas as pl
from jax.experimental.pallas import tpu as pltpu
from jax.sharding import PartitionSpec as P

LANES = 128
MIB = 1024 * 1024


def dot(a, b, dims=((1,), (0,))):
    return lax.dot_general(a, b, (dims, ((), ())), preferred_element_type=jnp.float32)


def after(x, *earlier):
    return lax.optimization_barrier((x,) + earlier)[0]


def pick_rows(pick, pieces, extra=None):
    slots, tokens = pick.shape
    width = pieces[0].shape[1]
    more = 0 if extra is None else extra.shape[1]
    extras = [] if extra is None else [extra]
    step = 512

    def kernel(pick_ref, *refs):
        piece_refs, extra_refs = refs[: len(pieces)], refs[len(pieces) : len(pieces) + len(extras)]
        out_ref, rows_ref = refs[-2:]
        at = 0
        for ref in piece_refs:
            rows_ref[at : at + ref.shape[0], :] = ref[...]
            at += ref.shape[0]
        for col in range(0, width, step):
            out_ref[:, col : col + step] = dot(
                pick_ref[...], rows_ref[:, col : col + step]
            ).astype(out_ref.dtype)
        for ref in extra_refs:
            out_ref[:, width:] = dot(pick_ref[...], ref[...]).astype(out_ref.dtype)

    return pl.pallas_call(
        kernel,
        out_shape=jax.ShapeDtypeStruct((slots, width + more), jnp.bfloat16),
        scratch_shapes=[pltpu.VMEM((tokens, width), jnp.bfloat16)],
        compiler_params=pltpu.CompilerParams(vmem_limit_bytes=16 * MIB),
        cost_estimate=pl.CostEstimate(
            flops=2 * slots * tokens * (width + more),
            bytes_accessed=2 * (slots + tokens) * (width + more),
            transcendentals=0,
        ),
        name="pick_rows",
    )(pick, *pieces, *extras)


def backward_rows(gr_rows, forward, downs, ins, mark):
    rows2, half = gr_rows.shape
    rows = rows2 // 2
    hid = downs[0].shape[0]
    width = 2 * half
    chunk = 1024
    tile = 256
    chunks = width // chunk
    n_in = len(ins)

    def kernel(mark_ref, gr_hbm, *refs):
        fwd_hbm, refs = refs[:6], refs[6:]
        down_hbm, refs = refs[:2], refs[2:]
        in_hbm, refs = refs[:n_in], refs[n_in:]
        out_ref, gr_ref, down_ref, fwd_ref, in_ref, grads_ref, *refs = refs
        gr_sem, down_sem, fwd_sem, in_sem = refs
        fwd_copies = [
            pltpu.make_async_copy(fwd_hbm[w], fwd_ref.at[w], fwd_sem.at[w]) for w in range(6)
        ]
        gr_copies, down_copies, in_copies = [], [], []
        for h in range(2):
            at = pl.ds(h * rows, rows)
            gr_copies.append(pltpu.make_async_copy(gr_hbm.at[at], gr_ref.at[at], gr_sem.at[h]))
            for w in range(2):
                cols = pl.ds(h * half, half)
                down_copies.append(
                    pltpu.make_async_copy(
                        down_hbm[w].at[:, cols],
                        down_ref.at[pl.ds(w * hid, hid), cols],
                        down_sem.at[2 * h + w],
                    )
                )
        for c in range(chunks):
            at = pl.ds(c * chunk, chunk)
            for w in range(n_in):
                in_copies.append(
                    pltpu.make_async_copy(
                        in_hbm[w].at[at],
                        in_ref.at[at, pl.ds(w * hid, hid)],
                        in_sem.at[c * n_in + w],
                    )
                )
        for h in range(2):
            gr_copies[h].start()
            down_copies[2 * h].start()
            down_copies[2 * h + 1].start()
        for copy in fwd_copies + in_copies:
            copy.start()

        last = ((1,), (1,))
        total = None
        for h in range(2):
            gr_copies[h].wait()
            down_copies[2 * h].wait()
            down_copies[2 * h + 1].wait()
            part = dot(
                gr_ref[h * rows : (h + 1) * rows, :],
                down_ref[:, h * half : (h + 1) * half],
                last,
            )
            total = part if total is None else total + part
        prob = jnp.zeros((rows, 1), jnp.float32)
        for w in range(2):
            for copy in fwd_copies[3 * w : 3 * w + 3]:
                copy.wait()
            act, to_gate, to_up = (fwd_ref[i] for i in range(3 * w, 3 * w + 3))
            hidden_grad = total[:, w * hid : (w + 1) * hid]
            prob = prob + jnp.sum(hidden_grad * act, axis=1, keepdims=True)
            at = 2 * w * hid
            grads_ref[:, at : at + hid] = (hidden_grad * to_gate).astype(jnp.bfloat16)
            grads_ref[:, at + hid : at + 2 * hid] = (hidden_grad * to_up).astype(jnp.bfloat16)
        lane = lax.broadcasted_iota(jnp.int32, (rows, LANES), 1)
        marked = jnp.where(lane == mark_ref[0], prob, 0.0).astype(jnp.bfloat16)
        for h in range(2):
            out_ref[h * rows : (h + 1) * rows, half:] = marked
        for c in range(chunks):
            for copy in in_copies[c * n_in : (c + 1) * n_in]:
                copy.wait()
            h, first = divmod(c * chunk, half)
            for col in range(0, chunk, tile):
                weights = in_ref[c * chunk + col : c * chunk + col + tile, :]
                out_ref[h * rows : (h + 1) * rows, first + col : first + col + tile] = dot(
                    grads_ref[...], weights, last
                ).astype(jnp.bfloat16)

    vmem, hbm = pl.BlockSpec(memory_space=pltpu.VMEM), pl.BlockSpec(memory_space=pl.ANY)
    return pl.pallas_call(
        kernel,
        out_shape=jax.ShapeDtypeStruct((rows2, half + LANES), jnp.bfloat16),
        in_specs=[pl.BlockSpec(memory_space=pltpu.SMEM), hbm]
        + [hbm] * (8 + n_in),
        out_specs=vmem,
        scratch_shapes=[
            pltpu.VMEM((rows2, half), jnp.bfloat16),
            pltpu.VMEM((2 * hid, width), jnp.bfloat16),
            pltpu.VMEM((6, rows, hid), jnp.float32),
            pltpu.VMEM((width, n_in * hid), jnp.bfloat16),
            pltpu.VMEM((rows, n_in * hid), jnp.bfloat16),
            pltpu.SemaphoreType.DMA((2,)),
            pltpu.SemaphoreType.DMA((4,)),
            pltpu.SemaphoreType.DMA((6,)),
            pltpu.SemaphoreType.DMA((chunks * n_in,)),
        ],
        compiler_params=pltpu.CompilerParams(vmem_limit_bytes=36 * MIB),
        cost_estimate=pl.CostEstimate(
            flops=2 * rows * width * 6 * hid,
            bytes_accessed=2 * width * 6 * hid + 8 * rows2 * half,
            transcendentals=0,
        ),
        name="backward_rows",
    )(mark, gr_rows, *forward, *downs, *ins)


def outer_sum(act, gr_rows, added=None):
    rows, hid = act.shape
    half = gr_rows.shape[1]
    step = 512

    def kernel(act_ref, gr_ref, *refs):
        out_ref = refs[-1]
        for h in range(2):
            for col in range(0, half, step):
                value = dot(
                    act_ref[...],
                    gr_ref[h * rows : (h + 1) * rows, col : col + step],
                    ((0,), (0,)),
                )
                at = h * half + col
                if added is not None:
                    value = value + refs[0][:, at : at + step].astype(jnp.float32)
                out_ref[:, at : at + step] = value.astype(jnp.bfloat16)

    return pl.pallas_call(
        kernel,
        out_shape=jax.ShapeDtypeStruct((hid, 2 * half), jnp.bfloat16),
        compiler_params=pltpu.CompilerParams(vmem_limit_bytes=16 * MIB),
        cost_estimate=pl.CostEstimate(
            flops=4 * rows * half * hid, bytes_accessed=8 * hid * half, transcendentals=0
        ),
        name="outer_sum",
    )(act, gr_rows, *([] if added is None else [added]))


def body(layer_input, out_grad, gate_prob, expert_ids, gate_weight, up_weight, down_weight):
    bf16, f32 = jnp.bfloat16, jnp.float32
    tok_rows, choose = expert_ids.shape
    half = layer_input.shape[1]
    n_high, n_low, n_core = lax.axis_size("ex"), lax.axis_size("ey"), lax.axis_size("tp")
    experts = n_high * n_low
    capacity = 3 * tok_rows * choose // (2 * experts) * n_high
    share = capacity // n_core
    tokens = tok_rows * n_high
    slots = n_low * capacity
    rows = slots // n_core
    high, low = lax.axis_index("ex"), lax.axis_index("ey")
    swap = [(0, 1), (1, 0)]
    far = n_high // 2
    mid = tok_rows // 2

    def across(x):
        return lax.all_to_all(x, ("tp", "ey"), split_axis=0, concat_axis=0, tiled=True)

    def swapped(x):
        return lax.ppermute(x, "tp", swap)

    def upward(x):
        return lax.ppermute(x, "ex", [(i, (i + 1) % n_high) for i in range(n_high)])

    def downward(x):
        return lax.ppermute(x, "ex", [(i, (i - 1) % n_high) for i in range(n_high)])

    def gathered(x):
        ups, downs = [x], [x]
        for _ in range(far - 1):
            ups.append(upward(ups[-1]))
            downs.append(downward(downs[-1]))
        opposite = [upward(ups[-1][:mid]), downward(downs[-1][mid:])]
        return downs + opposite + ups[:0:-1]

    def scattered(block, beside):
        opposite = block(far)
        up, down = upward(opposite[:mid]), downward(opposite[mid:])
        for i in range(far - 1, 0, -1):
            ahead, behind = block(i), block(n_high - i)
            if i == far - 1:
                ahead = jnp.concatenate(
                    [(ahead[:mid].astype(f32) + up.astype(f32)).astype(bf16), ahead[mid:]], axis=0
                )
                behind = jnp.concatenate(
                    [behind[:mid], (behind[mid:].astype(f32) + down.astype(f32)).astype(bf16)],
                    axis=0,
                )
            else:
                ahead = (ahead.astype(f32) + up.astype(f32)).astype(bf16)
                behind = (behind.astype(f32) + down.astype(f32)).astype(bf16)
            ahead, behind = beside(i, ahead, behind)
            up, down = upward(ahead), downward(behind)
        return up, down

    meta = jnp.concatenate(
        [expert_ids.astype(bf16), gate_prob, jnp.zeros((tok_rows, LANES - 2 * choose), bf16)],
        axis=1,
    )
    metas = lax.all_to_all(
        jnp.broadcast_to(meta[None], (n_high, tok_rows, LANES)), "ex", 0, 0, tiled=True
    ).reshape(tokens, LANES)
    metas = lax.dynamic_slice_in_dim(
        jnp.concatenate([metas, metas], axis=0), high * tok_rows, tokens, 0
    )
    metas_t = metas[:, : 2 * choose].astype(f32).T
    all_ids = metas_t[:choose].astype(jnp.int32)
    all_probs = metas_t[choose:]

    mine = lax.broadcasted_iota(jnp.int32, (n_low, 1, 1), 0) + high * n_low
    named = all_ids[None, :, :] == mine
    chosen = jnp.sum(named.astype(f32), axis=1)
    weight = jnp.sum(jnp.where(named, all_probs[None], 0.0), axis=1)
    earlier = (
        lax.broadcasted_iota(jnp.int32, (tokens, tokens), 0)
        < lax.broadcasted_iota(jnp.int32, (tokens, tokens), 1)
    ).astype(bf16)
    rank = dot(chosen.astype(bf16), earlier).astype(jnp.int32)
    rank = jnp.where(chosen > 0, rank, -1)
    place = lax.broadcasted_iota(jnp.int32, (n_core, 1, share, 1), 0) * share
    place = place + lax.broadcasted_iota(jnp.int32, (n_core, 1, share, 1), 2)
    pick = (rank[None, :, None, :] == place).astype(bf16).reshape(slots, tokens)
    pick = lax.optimization_barrier(pick)
    lane = lax.broadcasted_iota(jnp.int32, (1, LANES), 1)
    weights = jnp.concatenate([weight, jnp.zeros((LANES - n_low, tokens), f32)], axis=0)
    weights = weights.T.astype(bf16)

    all_inputs = gathered(layer_input)
    send_inputs = pick_rows(pick, all_inputs, weights)
    gate_own, up_own, down_own, out_grad = lax.optimization_barrier(
        (gate_weight[0], up_weight[0], down_weight[0], after(out_grad, send_inputs))
    )
    in_rows = across(send_inputs)
    gate_other, up_other, down_other = swapped(gate_own), swapped(up_own), swapped(down_own)
    send_grads = pick_rows(pick, gathered(out_grad))
    in_rows, send_grads = lax.optimization_barrier((in_rows, send_grads))
    gr_rows = across(send_grads)

    route_weight = jnp.sum(
        jnp.where(lane == low, in_rows[:rows, half:].astype(f32), 0.0), axis=1, keepdims=True
    )
    in0, in1 = in_rows[:rows, :half], in_rows[rows:, :half]
    forward, acts = [], []
    for gate_w, up_w in ((gate_own, up_own), (gate_other, up_other)):
        gate_pre = dot(in0, gate_w[:half]) + dot(in1, gate_w[half:])
        up_pre = dot(in0, up_w[:half]) + dot(in1, up_w[half:])
        gate_sigmoid = jax.nn.sigmoid(gate_pre)
        silu_gate = gate_pre * gate_sigmoid
        hidden_act = silu_gate * up_pre
        to_gate = route_weight * up_pre * gate_sigmoid * (1.0 + gate_pre * (1.0 - gate_sigmoid))
        to_up = route_weight * silu_gate
        forward += [hidden_act, to_gate, to_up]
        acts.append((route_weight * hidden_act).astype(bf16))
    gr_rows, forward, acts = lax.optimization_barrier((gr_rows, forward, acts))

    mark = jnp.reshape(high * n_low + low, (1,)).astype(jnp.int32)
    back = backward_rows(
        gr_rows,
        forward,
        (down_own, down_other),
        (gate_own, up_own, gate_other, up_other),
        mark,
    )
    home = across(back)

    sums = dot(pick, home, ((0,), (0,))).astype(bf16)
    sums, acts = lax.optimization_barrier((sums, acts))
    made = {}

    def beside(i, ahead, behind):
        if i == far - 1:
            there = outer_sum(acts[1], gr_rows)
            ahead, behind, there = lax.optimization_barrier((ahead, behind, there))
            made["there"] = swapped(there)
        if i == 1:
            made["down"] = outer_sum(acts[0], gr_rows, made["there"])
            ahead, behind, made["down"] = lax.optimization_barrier((ahead, behind, made["down"]))
        return ahead, behind

    def block(i):
        return sums[i * tok_rows : (i + 1) * tok_rows]

    up, down = scattered(block, beside)
    final = block(0).astype(f32) + up.astype(f32) + down.astype(f32)
    input_grad = final[:, :half].astype(bf16)
    found = jnp.sum(
        jnp.where(expert_ids[:, :, None] == lane[None], final[:, None, half:], 0.0), axis=2
    )
    return (input_grad, found.astype(bf16), made["down"][None])


def solution(mesh):
    return jax.shard_map(
        body,
        mesh=mesh,
        in_specs=(
            P(("ex", "ey"), "tp"),
            P(("ex", "ey"), "tp"),
            P(("ex", "ey"), None),
            P(("ex", "ey"), None),
            P(("ex", "ey"), None, "tp"),
            P(("ex", "ey"), None, "tp"),
            P(("ex", "ey"), "tp", None),
        ),
        out_specs=(P(("ex", "ey"), "tp"), P(("ex", "ey"), None), P(("ex", "ey"), "tp", None)),
        check_vma=False,
    )
```

```python
import jax
import jax.numpy as jnp
from jax import lax
from jax.experimental import pallas as pl
from jax.experimental.pallas import tpu as pltpu
from jax.sharding import PartitionSpec as P

LANES = 128
MIB = 1024 * 1024


def dot(a, b, dims=((1,), (0,))):
    return lax.dot_general(a, b, (dims, ((), ())), preferred_element_type=jnp.float32)


def after(x, *earlier):
    return lax.optimization_barrier((x,) + earlier)[0]


def pick_rows(pick, pieces, extra=None):
    slots, tokens = pick.shape
    width = pieces[0].shape[1]
    more = 0 if extra is None else extra.shape[1]
    extras = [] if extra is None else [extra]
    step = 512
    spans = [(at, step) for at in range(0, width, step)] + [(width, more)] * len(extras)

    def kernel(pick_ref, *refs):
        piece_refs, extra_refs = refs[: len(pieces)], refs[len(pieces) : len(pieces) + len(extras)]
        out_hbm, rows_ref, out_ref, sem = refs[-4:]
        at = 0
        for ref in piece_refs:
            rows_ref[at : at + ref.shape[0], :] = ref[...]
            at += ref.shape[0]
        copies = []
        for i, (col, size) in enumerate(spans):
            source = rows_ref[:, col : col + size] if col < width else extra_refs[0][...]
            out_ref[:, col : col + size] = dot(pick_ref[...], source).astype(out_ref.dtype)
            cols = pl.ds(col, size)
            copies.append(
                pltpu.make_async_copy(out_ref.at[:, cols], out_hbm.at[:, cols], sem.at[i])
            )
            copies[-1].start()
        for copy in copies:
            copy.wait()

    return pl.pallas_call(
        kernel,
        out_shape=jax.ShapeDtypeStruct((slots, width + more), jnp.bfloat16),
        out_specs=pl.BlockSpec(memory_space=pltpu.HBM),
        scratch_shapes=[
            pltpu.VMEM((tokens, width), jnp.bfloat16),
            pltpu.VMEM((slots, width + more), jnp.bfloat16),
            pltpu.SemaphoreType.DMA((len(spans),)),
        ],
        compiler_params=pltpu.CompilerParams(vmem_limit_bytes=16 * MIB),
        cost_estimate=pl.CostEstimate(
            flops=2 * slots * tokens * (width + more),
            bytes_accessed=2 * (slots + tokens) * (width + more),
            transcendentals=0,
        ),
        name="pick_rows",
    )(pick, *pieces, *extras)


def backward_rows(gr_rows, forward, downs, ins, mark):
    rows2, half = gr_rows.shape
    rows = rows2 // 2
    hid = downs[0].shape[0]
    width = 2 * half
    chunk = 1024
    tile = 256
    chunks = width // chunk
    n_in = len(ins)

    def kernel(mark_ref, gr_hbm, *refs):
        fwd_hbm, refs = refs[0], refs[1:]
        down_hbm, refs = refs[:2], refs[2:]
        in_hbm, refs = refs[:n_in], refs[n_in:]
        out_hbm, gr_ref, down_ref, fwd_ref, in_ref, grads_ref, out_ref, *refs = refs
        gr_sem, down_sem, fwd_sem, in_sem, out_sem = refs
        fwd_copy = pltpu.make_async_copy(fwd_hbm, fwd_ref, fwd_sem)
        gr_copies, down_copies, in_copies = [], [], []
        for h in range(2):
            at = pl.ds(h * rows, rows)
            gr_copies.append(pltpu.make_async_copy(gr_hbm.at[at], gr_ref.at[at], gr_sem.at[h]))
            for w in range(2):
                cols = pl.ds(h * half, half)
                down_copies.append(
                    pltpu.make_async_copy(
                        down_hbm[w].at[:, cols],
                        down_ref.at[pl.ds(w * hid, hid), cols],
                        down_sem.at[2 * h + w],
                    )
                )
        for c in range(chunks):
            at = pl.ds(c * chunk, chunk)
            for w in range(n_in):
                in_copies.append(
                    pltpu.make_async_copy(
                        in_hbm[w].at[at],
                        in_ref.at[at, pl.ds(w * hid, hid)],
                        in_sem.at[c * n_in + w],
                    )
                )
        for h in range(2):
            gr_copies[h].start()
            down_copies[2 * h].start()
            down_copies[2 * h + 1].start()
        fwd_copy.start()

        last = ((1,), (1,))
        total = None
        for h in range(2):
            gr_copies[h].wait()
            down_copies[2 * h].wait()
            down_copies[2 * h + 1].wait()
            part = dot(
                gr_ref[h * rows : (h + 1) * rows, :],
                down_ref[:, h * half : (h + 1) * half],
                last,
            )
            if h == 0:
                for copy in in_copies[:n_in]:
                    copy.start()
            else:
                fwd_copy.wait()
                for copy in in_copies[n_in:]:
                    copy.start()
            total = part if total is None else total + part
        prob = jnp.zeros((rows, 1), jnp.float32)
        for w in range(2):
            act, to_gate, to_up = (fwd_ref[i] for i in range(3 * w, 3 * w + 3))
            hidden_grad = total[:, w * hid : (w + 1) * hid]
            prob = prob + jnp.sum(hidden_grad * act, axis=1, keepdims=True)
            at = 2 * w * hid
            grads_ref[:, at : at + hid] = (hidden_grad * to_gate).astype(jnp.bfloat16)
            grads_ref[:, at + hid : at + 2 * hid] = (hidden_grad * to_up).astype(jnp.bfloat16)
        lane = lax.broadcasted_iota(jnp.int32, (rows, LANES), 1)
        marked = jnp.where(lane == mark_ref[0], prob, 0.0).astype(jnp.bfloat16)
        out_copies = []

        def send(h, first, size):
            span = (pl.ds(h * rows, rows), pl.ds(first, size))
            out_copies.append(
                pltpu.make_async_copy(
                    out_ref.at[span], out_hbm.at[span], out_sem.at[len(out_copies)]
                )
            )
            out_copies[-1].start()

        for h in range(2):
            out_ref[h * rows : (h + 1) * rows, half:] = marked
            send(h, half, LANES)
        for c in range(chunks):
            for copy in in_copies[c * n_in : (c + 1) * n_in]:
                copy.wait()
            h, first = divmod(c * chunk, half)
            for col in range(0, chunk, tile):
                weights = in_ref[c * chunk + col : c * chunk + col + tile, :]
                out_ref[h * rows : (h + 1) * rows, first + col : first + col + tile] = dot(
                    grads_ref[...], weights, last
                ).astype(jnp.bfloat16)
            send(h, first, chunk)
        for copy in out_copies:
            copy.wait()

    hbm = pl.BlockSpec(memory_space=pltpu.HBM)
    return pl.pallas_call(
        kernel,
        out_shape=jax.ShapeDtypeStruct((rows2, half + LANES), jnp.bfloat16),
        in_specs=[
            pl.BlockSpec(memory_space=pltpu.SMEM),
            pl.BlockSpec(memory_space=pl.ANY),
        ]
        + [hbm] * (3 + n_in),
        out_specs=hbm,
        scratch_shapes=[
            pltpu.VMEM((rows2, half), jnp.bfloat16),
            pltpu.VMEM((2 * hid, width), jnp.bfloat16),
            pltpu.VMEM((6, rows, hid), jnp.float32),
            pltpu.VMEM((width, n_in * hid), jnp.bfloat16),
            pltpu.VMEM((rows, n_in * hid), jnp.bfloat16),
            pltpu.VMEM((rows2, half + LANES), jnp.bfloat16),
            pltpu.SemaphoreType.DMA((2,)),
            pltpu.SemaphoreType.DMA((4,)),
            pltpu.SemaphoreType.DMA,
            pltpu.SemaphoreType.DMA((chunks * n_in,)),
            pltpu.SemaphoreType.DMA((chunks + 2,)),
        ],
        compiler_params=pltpu.CompilerParams(vmem_limit_bytes=60 * MIB),
        cost_estimate=pl.CostEstimate(
            flops=2 * rows * width * 6 * hid,
            bytes_accessed=2 * width * 6 * hid + 8 * rows2 * half,
            transcendentals=0,
        ),
        name="backward_rows",
    )(mark, gr_rows, forward, *downs, *ins)


def outer_sum(acts, grads, h, into=None):
    rows, hid = acts[0].shape
    half = grads[0].shape[1]
    step = 512
    n = len(acts)
    old = [] if into is None else [into]

    def kernel(*refs):
        act_refs, gr_refs = refs[:n], refs[n : 2 * n]
        out_hbm, out_ref, sem = refs[-3:]
        copies = []
        for i, col in enumerate(range(0, half, step)):
            value = sum(
                dot(a[...], g[:, col : col + step], ((0,), (0,)))
                for a, g in zip(act_refs, gr_refs)
            )
            out_ref[:, col : col + step] = value.astype(jnp.bfloat16)
            copies.append(
                pltpu.make_async_copy(
                    out_ref.at[:, pl.ds(col, step)],
                    out_hbm.at[:, pl.ds(h * half + col, step)],
                    sem.at[i],
                )
            )
            copies[-1].start()
        for copy in copies:
            copy.wait()

    return pl.pallas_call(
        kernel,
        out_shape=jax.ShapeDtypeStruct((hid, 2 * half), jnp.bfloat16),
        grid=(1,),
        in_specs=[pl.BlockSpec((rows, hid), lambda i: (0, 0))] * n
        + [pl.BlockSpec((rows, half), lambda i: (h, 0))] * n
        + [pl.BlockSpec(memory_space=pltpu.HBM)] * len(old),
        out_specs=pl.BlockSpec(memory_space=pltpu.HBM),
        scratch_shapes=[
            pltpu.VMEM((hid, half), jnp.bfloat16),
            pltpu.SemaphoreType.DMA((half // step,)),
        ],
        input_output_aliases={2 * n: 0} if old else {},
        compiler_params=pltpu.CompilerParams(vmem_limit_bytes=24 * MIB),
        cost_estimate=pl.CostEstimate(
            flops=4 * rows * half * hid, bytes_accessed=6 * hid * half, transcendentals=0
        ),
        name="outer_sum",
    )(*acts, *grads, *old)


def body(layer_input, out_grad, gate_prob, expert_ids, gate_weight, up_weight, down_weight):
    bf16, f32 = jnp.bfloat16, jnp.float32
    tok_rows, choose = expert_ids.shape
    half = layer_input.shape[1]
    n_high, n_low, n_core = lax.axis_size("ex"), lax.axis_size("ey"), lax.axis_size("tp")
    experts = n_high * n_low
    capacity = 3 * tok_rows * choose // (2 * experts) * n_high
    share = capacity // n_core
    tokens = tok_rows * n_high
    slots = n_low * capacity
    rows = slots // n_core
    high, low = lax.axis_index("ex"), lax.axis_index("ey")
    swap = [(0, 1), (1, 0)]
    far = n_high // 2
    mid = tok_rows // 2

    def across(x):
        return lax.all_to_all(x, ("tp", "ey"), split_axis=0, concat_axis=0, tiled=True)

    def swapped(x):
        return lax.ppermute(x, "tp", swap)

    def upward(x):
        return lax.ppermute(x, "ex", [(i, (i + 1) % n_high) for i in range(n_high)])

    def downward(x):
        return lax.ppermute(x, "ex", [(i, (i - 1) % n_high) for i in range(n_high)])

    def gathered(x):
        ups, downs = [x], [x]
        for _ in range(far - 1):
            ups.append(upward(ups[-1]))
            downs.append(downward(downs[-1]))
        opposite = [upward(ups[-1][:mid]), downward(downs[-1][mid:])]
        return downs + opposite + ups[:0:-1]

    def scattered(block, beside):
        opposite = block(far)
        up, down = upward(opposite[:mid]), downward(opposite[mid:])
        for i in range(far - 1, 0, -1):
            up, down = lax.optimization_barrier((up, down))
            ahead, behind = block(i), block(n_high - i)
            if i == far - 1:
                ahead = jnp.concatenate(
                    [(ahead[:mid].astype(f32) + up.astype(f32)).astype(bf16), ahead[mid:]], axis=0
                )
                behind = jnp.concatenate(
                    [behind[:mid], (behind[mid:].astype(f32) + down.astype(f32)).astype(bf16)],
                    axis=0,
                )
            else:
                ahead = (ahead.astype(f32) + up.astype(f32)).astype(bf16)
                behind = (behind.astype(f32) + down.astype(f32)).astype(bf16)
            ahead, behind = beside(i, ahead, behind)
            up, down = upward(ahead), downward(behind)
        return up, down

    meta = jnp.concatenate([expert_ids.T.astype(bf16), gate_prob.T], axis=0)
    meta = jnp.pad(meta, ((0, 0), (0, LANES - tok_rows)))
    metas = lax.all_to_all(
        jnp.broadcast_to(meta[None], (n_high,) + meta.shape), "ex", 0, 0, tiled=True
    )
    metas = lax.dynamic_slice_in_dim(jnp.concatenate([metas, metas], axis=0), high, n_high, 0)
    metas = metas[:, :, :tok_rows].astype(f32).transpose(1, 0, 2).reshape(2 * choose, tokens)
    all_ids = metas[:choose].astype(jnp.int32)
    all_probs = metas[choose:]

    mine = lax.broadcasted_iota(jnp.int32, (n_low, 1, 1), 0) + high * n_low
    named = all_ids[None, :, :] == mine
    chosen = jnp.sum(named.astype(f32), axis=1)
    weight = jnp.sum(jnp.where(named, all_probs[None], 0.0), axis=1)
    earlier = (
        lax.broadcasted_iota(jnp.int32, (tokens, tokens), 0)
        < lax.broadcasted_iota(jnp.int32, (tokens, tokens), 1)
    ).astype(bf16)
    rank = dot(chosen.astype(bf16), earlier).astype(jnp.int32)
    rank = jnp.where(chosen > 0, rank, -1)
    place = lax.broadcasted_iota(jnp.int32, (n_core, 1, share, 1), 0) * share
    place = place + lax.broadcasted_iota(jnp.int32, (n_core, 1, share, 1), 2)
    pick = (rank[None, :, None, :] == place).astype(bf16).reshape(slots, tokens)
    pick = lax.optimization_barrier(pick)
    lane = lax.broadcasted_iota(jnp.int32, (1, LANES), 1)
    weights = jnp.concatenate([weight, jnp.zeros((LANES - n_low, tokens), f32)], axis=0)
    weights = weights.T.astype(bf16)

    all_inputs = gathered(layer_input)
    send_inputs = pick_rows(pick, all_inputs, weights)
    gate_own, up_own, down_own = gate_weight[0], up_weight[0], down_weight[0]
    out_grad = after(out_grad, send_inputs)
    in_rows = across(send_inputs)
    gate_other, up_other, down_other = swapped(gate_own), swapped(up_own), swapped(down_own)
    send_grads = pick_rows(pick, gathered(out_grad))
    in_rows, send_grads = lax.optimization_barrier((in_rows, send_grads))
    gr_rows = across(send_grads)

    route_weight = jnp.sum(
        jnp.where(lane == low, in_rows[:rows, half:].astype(f32), 0.0), axis=1, keepdims=True
    )
    in0, in1 = in_rows[:rows, :half], in_rows[rows:, :half]
    forward, acts = [], []
    for gate_w, up_w in ((gate_own, up_own), (gate_other, up_other)):
        gate_pre = dot(in0, gate_w[:half]) + dot(in1, gate_w[half:])
        up_pre = dot(in0, up_w[:half]) + dot(in1, up_w[half:])
        gate_sigmoid = jax.nn.sigmoid(gate_pre)
        silu_gate = gate_pre * gate_sigmoid
        hidden_act = silu_gate * up_pre
        to_gate = route_weight * up_pre * gate_sigmoid * (1.0 + gate_pre * (1.0 - gate_sigmoid))
        to_up = route_weight * silu_gate
        forward += [hidden_act, to_gate, to_up]
        acts.append((route_weight * hidden_act).astype(bf16))
    forward = jnp.stack(forward)
    gr_rows, forward, acts = lax.optimization_barrier((gr_rows, forward, acts))

    mark = jnp.reshape(high * n_low + low, (1,)).astype(jnp.int32)
    back = backward_rows(
        gr_rows,
        forward,
        (down_own, down_other),
        (gate_own, up_own, gate_other, up_other),
        mark,
    )
    other_act, other_rows = swapped(acts[1]), swapped(gr_rows)
    back, other_act, other_rows = lax.optimization_barrier((back, other_act, other_rows))
    home = across(back)

    home, acts, other_act = lax.optimization_barrier((home, acts, other_act))
    opposite = dot(pick[:, far * tok_rows : (far + 1) * tok_rows], home, ((0,), (0,)))
    sums = dot(pick, home, ((0,), (0,))).astype(bf16)
    made = [None]

    def beside(i, ahead, behind):
        if i in (1, 2):
            made[0] = outer_sum((acts[0], other_act), (gr_rows, other_rows), 2 - i, made[0])
            ahead, behind, made[0] = lax.optimization_barrier((ahead, behind, made[0]))
        else:
            ahead, behind = lax.optimization_barrier((ahead, behind))
        return ahead, behind

    def block(i):
        if i == far:
            return opposite.astype(bf16)
        return sums[i * tok_rows : (i + 1) * tok_rows]

    up, down = scattered(block, beside)
    final = block(0).astype(f32) + up.astype(f32) + down.astype(f32)
    input_grad = final[:, :half].astype(bf16)
    found = jnp.sum(
        jnp.where(expert_ids[:, :, None] == lane[None], final[:, None, half:], 0.0), axis=2
    )
    return (input_grad, found.astype(bf16), made[0][None])


def solution(mesh):
    return jax.shard_map(
        body,
        mesh=mesh,
        in_specs=(
            P(("ex", "ey"), "tp"),
            P(("ex", "ey"), "tp"),
            P(("ex", "ey"), None),
            P(("ex", "ey"), None),
            P(("ex", "ey"), None, "tp"),
            P(("ex", "ey"), None, "tp"),
            P(("ex", "ey"), "tp", None),
        ),
        out_specs=(P(("ex", "ey"), "tp"), P(("ex", "ey"), None), P(("ex", "ey"), "tp", None)),
        check_vma=False,
    )
```

```python
import jax
import jax.numpy as jnp
from jax import lax
from jax.experimental import pallas as pl
from jax.experimental.pallas import tpu as pltpu
from jax.sharding import PartitionSpec as P

LANES = 128
MIB = 1024 * 1024


def dot(a, b, dims=((1,), (0,))):
    return lax.dot_general(a, b, (dims, ((), ())), preferred_element_type=jnp.float32)


def after(x, *earlier):
    return lax.optimization_barrier((x,) + earlier)[0]


def pick_rows(pick, pieces, extra=None):
    slots, tokens = pick.shape
    width = pieces[0].shape[1]
    more = 0 if extra is None else extra.shape[1]
    extras = [] if extra is None else [extra]
    step = 512

    def kernel(pick_ref, *refs):
        piece_refs, extra_refs = refs[: len(pieces)], refs[len(pieces) : len(pieces) + len(extras)]
        out_ref, rows_ref = refs[-2:]
        at = 0
        for ref in piece_refs:
            rows_ref[at : at + ref.shape[0], :] = ref[...]
            at += ref.shape[0]
        for col in range(0, width, step):
            out_ref[:, col : col + step] = dot(
                pick_ref[...], rows_ref[:, col : col + step]
            ).astype(out_ref.dtype)
        for ref in extra_refs:
            out_ref[:, width:] = dot(pick_ref[...], ref[...]).astype(out_ref.dtype)

    return pl.pallas_call(
        kernel,
        out_shape=jax.ShapeDtypeStruct((slots, width + more), jnp.bfloat16),
        scratch_shapes=[pltpu.VMEM((tokens, width), jnp.bfloat16)],
        compiler_params=pltpu.CompilerParams(vmem_limit_bytes=16 * MIB),
        cost_estimate=pl.CostEstimate(
            flops=2 * slots * tokens * (width + more),
            bytes_accessed=2 * (slots + tokens) * (width + more),
            transcendentals=0,
        ),
        name="pick_rows",
    )(pick, *pieces, *extras)


def id_table(ids, probs, copies):
    choose, tokens = ids.shape

    def kernel(ids_ref, probs_ref, out_ref):
        values = jnp.concatenate(
            [ids_ref[...].astype(jnp.float32), probs_ref[...].astype(jnp.float32)], axis=0
        ).astype(jnp.bfloat16)
        out_ref[...] = jnp.zeros(out_ref.shape, out_ref.dtype)
        for i in range(copies):
            out_ref[i, :, :tokens] = values

    return pl.pallas_call(
        kernel,
        out_shape=jax.ShapeDtypeStruct((copies, 2 * choose, LANES), jnp.bfloat16),
        compiler_params=pltpu.CompilerParams(vmem_limit_bytes=4 * MIB),
        name="id_table",
    )(ids, probs)


def last_sum(sums, up, down, ids):
    tok_rows, width = up.shape
    half = width - LANES
    choose = ids.shape[1]

    def kernel(sums_ref, up_ref, down_ref, ids_ref, grad_ref, prob_ref):
        def total(cols):
            return sum(ref[:, cols].astype(jnp.float32) for ref in (sums_ref, up_ref, down_ref))

        grad_ref[...] = total(slice(0, half)).astype(jnp.bfloat16)
        by_expert = total(slice(half, width))
        lane = lax.broadcasted_iota(jnp.int32, (tok_rows, LANES), 1)
        found = jnp.zeros((tok_rows, LANES), jnp.float32)
        for k in range(choose):
            value = jnp.sum(
                jnp.where(lane == ids_ref[:, k : k + 1], by_expert, 0.0), axis=1, keepdims=True
            )
            found = jnp.where(lane == k, value, found)
        prob_ref[...] = found.T[:choose].astype(jnp.bfloat16)

    def whole(shape):
        return pl.BlockSpec(shape, lambda i: (0, 0))

    return pl.pallas_call(
        kernel,
        grid=(1,),
        out_shape=(
            jax.ShapeDtypeStruct((tok_rows, half), jnp.bfloat16),
            jax.ShapeDtypeStruct((choose, tok_rows), jnp.bfloat16),
        ),
        in_specs=[whole((tok_rows, width))] * 3 + [whole((tok_rows, choose))],
        out_specs=(whole((tok_rows, half)), whole((choose, tok_rows))),
        compiler_params=pltpu.CompilerParams(vmem_limit_bytes=8 * MIB),
        name="last_sum",
    )(sums, up, down, ids)


def backward_rows(gr_rows, forward, downs, ins, mark):
    rows2, half = gr_rows.shape
    rows = rows2 // 2
    hid = downs[0].shape[0]
    width = 2 * half
    chunk = 1024
    tile = 256
    chunks = width // chunk
    n_in = len(ins)

    def kernel(mark_ref, gr_hbm, *refs):
        fwd_hbm, refs = refs[0], refs[1:]
        down_hbm, refs = refs[:2], refs[2:]
        in_hbm, refs = refs[:n_in], refs[n_in:]
        out_hbm, gr_ref, down_ref, fwd_ref, in_ref, grads_ref, out_ref, *refs = refs
        gr_sem, down_sem, fwd_sem, in_sem, out_sem = refs
        fwd_copy = pltpu.make_async_copy(fwd_hbm, fwd_ref, fwd_sem)
        gr_copies, down_copies, in_copies = [], [], []
        spans = []
        for h in range(2):
            for col in range(0, half, chunk):
                n = len(spans)
                spans.append((h, col))
                span = (pl.ds(h * rows, rows), pl.ds(col, chunk))
                gr_copies.append(
                    pltpu.make_async_copy(gr_hbm.at[span], gr_ref.at[span], gr_sem.at[n])
                )
                cols = pl.ds(h * half + col, chunk)
                for w in range(2):
                    down_copies.append(
                        pltpu.make_async_copy(
                            down_hbm[w].at[:, cols],
                            down_ref.at[pl.ds(w * hid, hid), cols],
                            down_sem.at[2 * n + w],
                        )
                    )
        for c in range(chunks):
            at = pl.ds(c * chunk, chunk)
            for w in range(n_in):
                in_copies.append(
                    pltpu.make_async_copy(
                        in_hbm[w].at[at],
                        in_ref.at[at, pl.ds(w * hid, hid)],
                        in_sem.at[c * n_in + w],
                    )
                )
        for n in range(len(spans)):
            gr_copies[n].start()
            down_copies[2 * n].start()
            down_copies[2 * n + 1].start()
        fwd_copy.start()

        last = ((1,), (1,))
        total = None
        for n, (h, col) in enumerate(spans):
            gr_copies[n].wait()
            down_copies[2 * n].wait()
            down_copies[2 * n + 1].wait()
            part = dot(
                gr_ref[h * rows : (h + 1) * rows, col : col + chunk],
                down_ref[:, h * half + col : h * half + col + chunk],
                last,
            )
            for copy in in_copies[n * n_in : (n + 1) * n_in]:
                copy.start()
            total = part if total is None else total + part
        fwd_copy.wait()
        prob = jnp.zeros((rows, 1), jnp.float32)
        for w in range(2):
            act, to_gate, to_up = (fwd_ref[i] for i in range(3 * w, 3 * w + 3))
            hidden_grad = total[:, w * hid : (w + 1) * hid]
            prob = prob + jnp.sum(hidden_grad * act, axis=1, keepdims=True)
            at = 2 * w * hid
            grads_ref[:, at : at + hid] = (hidden_grad * to_gate).astype(jnp.bfloat16)
            grads_ref[:, at + hid : at + 2 * hid] = (hidden_grad * to_up).astype(jnp.bfloat16)
        lane = lax.broadcasted_iota(jnp.int32, (rows, LANES), 1)
        marked = jnp.where(lane == mark_ref[0], prob, 0.0).astype(jnp.bfloat16)
        out_copies = []

        def send(h, first, size):
            span = (pl.ds(h * rows, rows), pl.ds(first, size))
            out_copies.append(
                pltpu.make_async_copy(
                    out_ref.at[span], out_hbm.at[span], out_sem.at[len(out_copies)]
                )
            )
            out_copies[-1].start()

        for h in range(2):
            out_ref[h * rows : (h + 1) * rows, half:] = marked
            send(h, half, LANES)
        for c in range(chunks):
            for copy in in_copies[c * n_in : (c + 1) * n_in]:
                copy.wait()
            h, first = divmod(c * chunk, half)
            for col in range(0, chunk, tile):
                weights = in_ref[c * chunk + col : c * chunk + col + tile, :]
                out_ref[h * rows : (h + 1) * rows, first + col : first + col + tile] = dot(
                    grads_ref[...], weights, last
                ).astype(jnp.bfloat16)
            send(h, first, chunk)
        for copy in out_copies:
            copy.wait()

    hbm = pl.BlockSpec(memory_space=pltpu.HBM)
    return pl.pallas_call(
        kernel,
        out_shape=jax.ShapeDtypeStruct((rows2, half + LANES), jnp.bfloat16),
        in_specs=[
            pl.BlockSpec(memory_space=pltpu.SMEM),
            pl.BlockSpec(memory_space=pl.ANY),
        ]
        + [hbm] * (3 + n_in),
        out_specs=hbm,
        scratch_shapes=[
            pltpu.VMEM((rows2, half), jnp.bfloat16),
            pltpu.VMEM((2 * hid, width), jnp.bfloat16),
            pltpu.VMEM((6, rows, hid), jnp.float32),
            pltpu.VMEM((width, n_in * hid), jnp.bfloat16),
            pltpu.VMEM((rows, n_in * hid), jnp.bfloat16),
            pltpu.VMEM((rows2, half + LANES), jnp.bfloat16),
            pltpu.SemaphoreType.DMA((chunks,)),
            pltpu.SemaphoreType.DMA((2 * chunks,)),
            pltpu.SemaphoreType.DMA,
            pltpu.SemaphoreType.DMA((chunks * n_in,)),
            pltpu.SemaphoreType.DMA((chunks + 2,)),
        ],
        compiler_params=pltpu.CompilerParams(vmem_limit_bytes=60 * MIB),
        cost_estimate=pl.CostEstimate(
            flops=2 * rows * width * 6 * hid,
            bytes_accessed=2 * width * 6 * hid + 8 * rows2 * half,
            transcendentals=0,
        ),
        name="backward_rows",
    )(mark, gr_rows, forward, *downs, *ins)


def outer_sum(acts, grads, h, into=None):
    rows, hid = acts[0].shape
    half = grads[0].shape[1]
    step = 512
    n = len(acts)
    old = [] if into is None else [into]

    def kernel(*refs):
        act_refs, gr_refs = refs[:n], refs[n : 2 * n]
        out_hbm, out_ref, sem = refs[-3:]
        copies = []
        for i, col in enumerate(range(0, half, step)):
            value = sum(
                dot(a[...], g[:, col : col + step], ((0,), (0,)))
                for a, g in zip(act_refs, gr_refs)
            )
            out_ref[:, col : col + step] = value.astype(jnp.bfloat16)
            copies.append(
                pltpu.make_async_copy(
                    out_ref.at[:, pl.ds(col, step)],
                    out_hbm.at[:, pl.ds(h * half + col, step)],
                    sem.at[i],
                )
            )
            copies[-1].start()
        for copy in copies:
            copy.wait()

    return pl.pallas_call(
        kernel,
        out_shape=jax.ShapeDtypeStruct((hid, 2 * half), jnp.bfloat16),
        grid=(1,),
        in_specs=[pl.BlockSpec((rows, hid), lambda i: (0, 0))] * n
        + [pl.BlockSpec((rows, half), lambda i: (h, 0))] * n
        + [pl.BlockSpec(memory_space=pltpu.HBM)] * len(old),
        out_specs=pl.BlockSpec(memory_space=pltpu.HBM),
        scratch_shapes=[
            pltpu.VMEM((hid, half), jnp.bfloat16),
            pltpu.SemaphoreType.DMA((half // step,)),
        ],
        input_output_aliases={2 * n: 0} if old else {},
        compiler_params=pltpu.CompilerParams(vmem_limit_bytes=24 * MIB),
        cost_estimate=pl.CostEstimate(
            flops=4 * rows * half * hid, bytes_accessed=6 * hid * half, transcendentals=0
        ),
        name="outer_sum",
    )(*acts, *grads, *old)


def body(layer_input, out_grad, gate_prob, expert_ids, gate_weight, up_weight, down_weight):
    bf16, f32 = jnp.bfloat16, jnp.float32
    tok_rows, choose = expert_ids.shape
    half = layer_input.shape[1]
    n_high, n_low, n_core = lax.axis_size("ex"), lax.axis_size("ey"), lax.axis_size("tp")
    experts = n_high * n_low
    capacity = 3 * tok_rows * choose // (2 * experts) * n_high
    share = capacity // n_core
    tokens = tok_rows * n_high
    slots = n_low * capacity
    rows = slots // n_core
    high, low = lax.axis_index("ex"), lax.axis_index("ey")
    swap = [(0, 1), (1, 0)]
    far = n_high // 2
    mid = tok_rows // 2

    def across(x):
        return lax.all_to_all(x, ("tp", "ey"), split_axis=0, concat_axis=0, tiled=True)

    def swapped(x):
        return lax.ppermute(x, "tp", swap)

    def upward(x):
        return lax.ppermute(x, "ex", [(i, (i + 1) % n_high) for i in range(n_high)])

    def downward(x):
        return lax.ppermute(x, "ex", [(i, (i - 1) % n_high) for i in range(n_high)])

    def gathered(x):
        ups, downs = [x], [x]
        for _ in range(far - 1):
            ups.append(upward(ups[-1]))
            downs.append(downward(downs[-1]))
        opposite = [upward(ups[-1][:mid]), downward(downs[-1][mid:])]
        return downs + opposite + ups[:0:-1]

    def scattered(block, beside):
        opposite = block(far)
        up, down = upward(opposite[:mid]), downward(opposite[mid:])
        for i in range(far - 1, 0, -1):
            up, down = lax.optimization_barrier((up, down))
            ahead, behind = block(i), block(n_high - i)
            if i == far - 1:
                ahead = jnp.concatenate(
                    [(ahead[:mid].astype(f32) + up.astype(f32)).astype(bf16), ahead[mid:]], axis=0
                )
                behind = jnp.concatenate(
                    [behind[:mid], (behind[mid:].astype(f32) + down.astype(f32)).astype(bf16)],
                    axis=0,
                )
            else:
                ahead = (ahead.astype(f32) + up.astype(f32)).astype(bf16)
                behind = (behind.astype(f32) + down.astype(f32)).astype(bf16)
            ahead, behind = beside(i, ahead, behind)
            up, down = upward(ahead), downward(behind)
        return up, down

    metas = lax.all_to_all(id_table(expert_ids.T, gate_prob.T, n_high), "ex", 0, 0, tiled=True)
    metas = lax.dynamic_slice_in_dim(jnp.concatenate([metas, metas], axis=0), high, n_high, 0)
    metas = metas[:, :, :tok_rows].astype(f32).transpose(1, 0, 2).reshape(2 * choose, tokens)
    all_ids = metas[:choose].astype(jnp.int32)
    all_probs = metas[choose:]

    mine = lax.broadcasted_iota(jnp.int32, (n_low, 1, 1), 0) + high * n_low
    named = all_ids[None, :, :] == mine
    chosen = jnp.sum(named.astype(f32), axis=1)
    weight = jnp.sum(jnp.where(named, all_probs[None], 0.0), axis=1)
    earlier = (
        lax.broadcasted_iota(jnp.int32, (tokens, tokens), 0)
        < lax.broadcasted_iota(jnp.int32, (tokens, tokens), 1)
    ).astype(bf16)
    rank = dot(chosen.astype(bf16), earlier).astype(jnp.int32)
    rank = jnp.where(chosen > 0, rank, -1)
    place = lax.broadcasted_iota(jnp.int32, (n_core, 1, share, 1), 0) * share
    place = place + lax.broadcasted_iota(jnp.int32, (n_core, 1, share, 1), 2)
    pick = (rank[None, :, None, :] == place).astype(bf16).reshape(slots, tokens)
    pick = lax.optimization_barrier(pick)
    lane = lax.broadcasted_iota(jnp.int32, (1, LANES), 1)
    weights = jnp.concatenate([weight, jnp.zeros((LANES - n_low, tokens), f32)], axis=0)
    weights = weights.T.astype(bf16)

    all_inputs = gathered(layer_input)
    send_inputs = pick_rows(pick, all_inputs, weights)
    gate_own, up_own, down_own = gate_weight[0], up_weight[0], down_weight[0]
    out_grad = after(out_grad, send_inputs)
    in_rows = across(send_inputs)
    gate_other, up_other, down_other = swapped(gate_own), swapped(up_own), swapped(down_own)
    send_grads = pick_rows(pick, gathered(out_grad))
    in_rows, send_grads = lax.optimization_barrier((in_rows, send_grads))
    gr_rows = across(send_grads)

    route_weight = jnp.sum(
        jnp.where(lane == low, in_rows[:rows, half:].astype(f32), 0.0), axis=1, keepdims=True
    )
    in0, in1 = in_rows[:rows, :half], in_rows[rows:, :half]
    forward, acts = [], []
    for gate_w, up_w in ((gate_own, up_own), (gate_other, up_other)):
        gate_pre = dot(in0, gate_w[:half]) + dot(in1, gate_w[half:])
        up_pre = dot(in0, up_w[:half]) + dot(in1, up_w[half:])
        gate_sigmoid = jax.nn.sigmoid(gate_pre)
        silu_gate = gate_pre * gate_sigmoid
        hidden_act = silu_gate * up_pre
        to_gate = route_weight * up_pre * gate_sigmoid * (1.0 + gate_pre * (1.0 - gate_sigmoid))
        to_up = route_weight * silu_gate
        forward += [hidden_act, to_gate, to_up]
        acts.append((route_weight * hidden_act).astype(bf16))
    forward = jnp.stack(forward)
    gr_rows, forward, acts = lax.optimization_barrier((gr_rows, forward, acts))

    mark = jnp.reshape(high * n_low + low, (1,)).astype(jnp.int32)
    back = backward_rows(
        gr_rows,
        forward,
        (down_own, down_other),
        (gate_own, up_own, gate_other, up_other),
        mark,
    )
    other_act, other_rows = swapped(acts[1]), swapped(gr_rows)
    back, other_act, other_rows = lax.optimization_barrier((back, other_act, other_rows))
    home = across(back)

    home, acts, other_act = lax.optimization_barrier((home, acts, other_act))
    opposite = dot(pick[:, far * tok_rows : (far + 1) * tok_rows], home, ((0,), (0,)))
    sums = dot(pick, home, ((0,), (0,))).astype(bf16)
    made = [None]

    def beside(i, ahead, behind):
        if i in (1, 2):
            made[0] = outer_sum((acts[0], other_act), (gr_rows, other_rows), 2 - i, made[0])
            ahead, behind, made[0] = lax.optimization_barrier((ahead, behind, made[0]))
        else:
            ahead, behind = lax.optimization_barrier((ahead, behind))
        return ahead, behind

    def block(i):
        if i == far:
            return opposite.astype(bf16)
        return sums[i * tok_rows : (i + 1) * tok_rows]

    up, down = scattered(block, beside)
    input_grad, prob_grad = last_sum(sums, up, down, expert_ids)
    return (input_grad, prob_grad.T, made[0][None])


def solution(mesh):
    return jax.shard_map(
        body,
        mesh=mesh,
        in_specs=(
            P(("ex", "ey"), "tp"),
            P(("ex", "ey"), "tp"),
            P(("ex", "ey"), None),
            P(("ex", "ey"), None),
            P(("ex", "ey"), None, "tp"),
            P(("ex", "ey"), None, "tp"),
            P(("ex", "ey"), "tp", None),
        ),
        out_specs=(P(("ex", "ey"), "tp"), P(("ex", "ey"), None), P(("ex", "ey"), "tp", None)),
        check_vma=False,
    )
```

```python
import jax
import jax.numpy as jnp
from jax import lax
from jax.experimental import pallas as pl
from jax.experimental.pallas import tpu as pltpu
from jax.sharding import PartitionSpec as P

LANES = 128
MIB = 1024 * 1024


def dot(a, b, dims=((1,), (0,))):
    return lax.dot_general(a, b, (dims, ((), ())), preferred_element_type=jnp.float32)


def after(x, *earlier):
    return lax.optimization_barrier((x,) + earlier)[0]


def pick_rows(pick, pieces, extra=None):
    slots, tokens = pick.shape
    width = pieces[0].shape[1]
    more = 0 if extra is None else extra.shape[1]
    extras = [] if extra is None else [extra]
    step = 512

    def kernel(pick_ref, *refs):
        piece_refs, extra_refs = refs[: len(pieces)], refs[len(pieces) : len(pieces) + len(extras)]
        out_ref, rows_ref = refs[-2:]
        at = 0
        for ref in piece_refs:
            rows_ref[at : at + ref.shape[0], :] = ref[...]
            at += ref.shape[0]
        for col in range(0, width, step):
            out_ref[:, col : col + step] = dot(
                pick_ref[...], rows_ref[:, col : col + step]
            ).astype(out_ref.dtype)
        for ref in extra_refs:
            out_ref[:, width:] = dot(pick_ref[...], ref[...]).astype(out_ref.dtype)

    return pl.pallas_call(
        kernel,
        out_shape=jax.ShapeDtypeStruct((slots, width + more), jnp.bfloat16),
        scratch_shapes=[pltpu.VMEM((tokens, width), jnp.bfloat16)],
        compiler_params=pltpu.CompilerParams(vmem_limit_bytes=16 * MIB),
        cost_estimate=pl.CostEstimate(
            flops=2 * slots * tokens * (width + more),
            bytes_accessed=2 * (slots + tokens) * (width + more),
            transcendentals=0,
        ),
        name="pick_rows",
    )(pick, *pieces, *extras)


def id_table(ids, probs, copies):
    choose, tokens = ids.shape

    def kernel(ids_hbm, probs_hbm, out_ref, ids_ref, probs_ref, sem):
        ids_copy = pltpu.make_async_copy(ids_hbm, ids_ref, sem.at[0])
        probs_copy = pltpu.make_async_copy(probs_hbm, probs_ref, sem.at[1])
        ids_copy.start()
        probs_copy.start()
        ids_copy.wait()
        probs_copy.wait()
        values = jnp.concatenate(
            [ids_ref[...].astype(jnp.float32), probs_ref[...].astype(jnp.float32)], axis=0
        ).astype(jnp.bfloat16)
        out_ref[...] = jnp.zeros(out_ref.shape, out_ref.dtype)
        for i in range(copies):
            out_ref[i, :, :tokens] = values

    return pl.pallas_call(
        kernel,
        out_shape=jax.ShapeDtypeStruct((copies, 2 * choose, LANES), jnp.bfloat16),
        in_specs=[pl.BlockSpec(memory_space=pl.ANY)] * 2,
        scratch_shapes=[
            pltpu.VMEM(ids.shape, ids.dtype),
            pltpu.VMEM(probs.shape, probs.dtype),
            pltpu.SemaphoreType.DMA((2,)),
        ],
        compiler_params=pltpu.CompilerParams(vmem_limit_bytes=60 * MIB),
        name="id_table",
    )(ids, probs)


def last_sum(sums, up, down, ids):
    tok_rows, width = up.shape
    half = width - LANES
    choose = ids.shape[1]

    def kernel(sums_ref, up_ref, down_ref, ids_ref, grad_ref, prob_ref):
        def total(cols):
            return sum(ref[:, cols].astype(jnp.float32) for ref in (sums_ref, up_ref, down_ref))

        grad_ref[...] = total(slice(0, half)).astype(jnp.bfloat16)
        by_expert = total(slice(half, width))
        lane = lax.broadcasted_iota(jnp.int32, (tok_rows, LANES), 1)
        found = jnp.zeros((tok_rows, LANES), jnp.float32)
        for k in range(choose):
            value = jnp.sum(
                jnp.where(lane == ids_ref[:, k : k + 1], by_expert, 0.0), axis=1, keepdims=True
            )
            found = jnp.where(lane == k, value, found)
        prob_ref[...] = found.T[:choose].astype(jnp.bfloat16)

    def whole(shape):
        return pl.BlockSpec(shape, lambda i: (0, 0))

    return pl.pallas_call(
        kernel,
        grid=(1,),
        out_shape=(
            jax.ShapeDtypeStruct((tok_rows, half), jnp.bfloat16),
            jax.ShapeDtypeStruct((choose, tok_rows), jnp.bfloat16),
        ),
        in_specs=[whole((tok_rows, width))] * 3 + [whole((tok_rows, choose))],
        out_specs=(whole((tok_rows, half)), whole((choose, tok_rows))),
        compiler_params=pltpu.CompilerParams(vmem_limit_bytes=8 * MIB),
        name="last_sum",
    )(sums, up, down, ids)


def backward_rows(gr_rows, forward, downs, ins, mark):
    rows2, half = gr_rows.shape
    rows = rows2 // 2
    hid = downs[0].shape[0]
    width = 2 * half
    chunk = 1024
    tile = 256
    chunks = width // chunk
    n_in = len(ins)

    def kernel(mark_ref, gr_hbm, *refs):
        fwd_hbm, refs = refs[0], refs[1:]
        down_hbm, refs = refs[:2], refs[2:]
        in_hbm, refs = refs[:n_in], refs[n_in:]
        out_hbm, gr_ref, down_ref, fwd_ref, in_ref, grads_ref, out_ref, *refs = refs
        gr_sem, down_sem, fwd_sem, in_sem, out_sem = refs
        fwd_copy = pltpu.make_async_copy(fwd_hbm, fwd_ref, fwd_sem)
        gr_copies, down_copies, in_copies = [], [], []
        spans = []
        for h in range(2):
            for col in range(0, half, chunk):
                n = len(spans)
                spans.append((h, col))
                span = (pl.ds(h * rows, rows), pl.ds(col, chunk))
                gr_copies.append(
                    pltpu.make_async_copy(gr_hbm.at[span], gr_ref.at[span], gr_sem.at[n])
                )
                cols = pl.ds(h * half + col, chunk)
                for w in range(2):
                    down_copies.append(
                        pltpu.make_async_copy(
                            down_hbm[w].at[:, cols],
                            down_ref.at[pl.ds(w * hid, hid), cols],
                            down_sem.at[2 * n + w],
                        )
                    )
        for c in range(chunks):
            at = pl.ds(c * chunk, chunk)
            for w in range(n_in):
                in_copies.append(
                    pltpu.make_async_copy(
                        in_hbm[w].at[at],
                        in_ref.at[at, pl.ds(w * hid, hid)],
                        in_sem.at[c * n_in + w],
                    )
                )
        for n in range(len(spans)):
            gr_copies[n].start()
            down_copies[2 * n].start()
            down_copies[2 * n + 1].start()
        fwd_copy.start()

        last = ((1,), (1,))
        total = None
        for n, (h, col) in enumerate(spans):
            gr_copies[n].wait()
            down_copies[2 * n].wait()
            down_copies[2 * n + 1].wait()
            part = dot(
                gr_ref[h * rows : (h + 1) * rows, col : col + chunk],
                down_ref[:, h * half + col : h * half + col + chunk],
                last,
            )
            for copy in in_copies[n * n_in : (n + 1) * n_in]:
                copy.start()
            total = part if total is None else total + part
        fwd_copy.wait()
        prob = jnp.zeros((rows, 1), jnp.float32)
        for w in range(2):
            act, to_gate, to_up = (fwd_ref[i] for i in range(3 * w, 3 * w + 3))
            hidden_grad = total[:, w * hid : (w + 1) * hid]
            prob = prob + jnp.sum(hidden_grad * act, axis=1, keepdims=True)
            at = 2 * w * hid
            grads_ref[:, at : at + hid] = (hidden_grad * to_gate).astype(jnp.bfloat16)
            grads_ref[:, at + hid : at + 2 * hid] = (hidden_grad * to_up).astype(jnp.bfloat16)
        lane = lax.broadcasted_iota(jnp.int32, (rows, LANES), 1)
        marked = jnp.where(lane == mark_ref[0], prob, 0.0).astype(jnp.bfloat16)
        out_copies = []

        def send(h, first, size):
            span = (pl.ds(h * rows, rows), pl.ds(first, size))
            out_copies.append(
                pltpu.make_async_copy(
                    out_ref.at[span], out_hbm.at[span], out_sem.at[len(out_copies)]
                )
            )
            out_copies[-1].start()

        for h in range(2):
            out_ref[h * rows : (h + 1) * rows, half:] = marked
            send(h, half, LANES)
        for c in range(chunks):
            for copy in in_copies[c * n_in : (c + 1) * n_in]:
                copy.wait()
            h, first = divmod(c * chunk, half)
            for col in range(0, chunk, tile):
                weights = in_ref[c * chunk + col : c * chunk + col + tile, :]
                out_ref[h * rows : (h + 1) * rows, first + col : first + col + tile] = dot(
                    grads_ref[...], weights, last
                ).astype(jnp.bfloat16)
            send(h, first, chunk)
        for copy in out_copies:
            copy.wait()

    hbm = pl.BlockSpec(memory_space=pltpu.HBM)
    return pl.pallas_call(
        kernel,
        out_shape=jax.ShapeDtypeStruct((rows2, half + LANES), jnp.bfloat16),
        in_specs=[
            pl.BlockSpec(memory_space=pltpu.SMEM),
            pl.BlockSpec(memory_space=pl.ANY),
        ]
        + [hbm] * (3 + n_in),
        out_specs=hbm,
        scratch_shapes=[
            pltpu.VMEM((rows2, half), jnp.bfloat16),
            pltpu.VMEM((2 * hid, width), jnp.bfloat16),
            pltpu.VMEM((6, rows, hid), jnp.float32),
            pltpu.VMEM((width, n_in * hid), jnp.bfloat16),
            pltpu.VMEM((rows, n_in * hid), jnp.bfloat16),
            pltpu.VMEM((rows2, half + LANES), jnp.bfloat16),
            pltpu.SemaphoreType.DMA((chunks,)),
            pltpu.SemaphoreType.DMA((2 * chunks,)),
            pltpu.SemaphoreType.DMA,
            pltpu.SemaphoreType.DMA((chunks * n_in,)),
            pltpu.SemaphoreType.DMA((chunks + 2,)),
        ],
        compiler_params=pltpu.CompilerParams(vmem_limit_bytes=50 * MIB),
        cost_estimate=pl.CostEstimate(
            flops=2 * rows * width * 6 * hid,
            bytes_accessed=2 * width * 6 * hid + 8 * rows2 * half,
            transcendentals=0,
        ),
        name="backward_rows",
    )(mark, gr_rows, forward, *downs, *ins)


def outer_sum(acts, grads, h, into=None):
    rows, hid = acts[0].shape
    half = grads[0].shape[1]
    step = 512
    n = len(acts)
    old = [] if into is None else [into]

    def kernel(*refs):
        act_refs, gr_refs = refs[:n], refs[n : 2 * n]
        out_hbm, out_ref, sem = refs[-3:]
        copies = []
        for i, col in enumerate(range(0, half, step)):
            value = sum(
                dot(a[...], g[:, col : col + step], ((0,), (0,)))
                for a, g in zip(act_refs, gr_refs)
            )
            out_ref[:, col : col + step] = value.astype(jnp.bfloat16)
            copies.append(
                pltpu.make_async_copy(
                    out_ref.at[:, pl.ds(col, step)],
                    out_hbm.at[:, pl.ds(h * half + col, step)],
                    sem.at[i],
                )
            )
            copies[-1].start()
        for copy in copies:
            copy.wait()

    return pl.pallas_call(
        kernel,
        out_shape=jax.ShapeDtypeStruct((hid, 2 * half), jnp.bfloat16),
        grid=(1,),
        in_specs=[pl.BlockSpec((rows, hid), lambda i: (0, 0))] * n
        + [pl.BlockSpec((rows, half), lambda i: (h, 0))] * n
        + [pl.BlockSpec(memory_space=pltpu.HBM)] * len(old),
        out_specs=pl.BlockSpec(memory_space=pltpu.HBM),
        scratch_shapes=[
            pltpu.VMEM((hid, half), jnp.bfloat16),
            pltpu.SemaphoreType.DMA((half // step,)),
        ],
        input_output_aliases={2 * n: 0} if old else {},
        compiler_params=pltpu.CompilerParams(vmem_limit_bytes=24 * MIB),
        cost_estimate=pl.CostEstimate(
            flops=4 * rows * half * hid, bytes_accessed=6 * hid * half, transcendentals=0
        ),
        name="outer_sum",
    )(*acts, *grads, *old)


def body(layer_input, out_grad, gate_prob, expert_ids, gate_weight, up_weight, down_weight):
    bf16, f32 = jnp.bfloat16, jnp.float32
    tok_rows, choose = expert_ids.shape
    half = layer_input.shape[1]
    n_high, n_low, n_core = lax.axis_size("ex"), lax.axis_size("ey"), lax.axis_size("tp")
    experts = n_high * n_low
    capacity = 3 * tok_rows * choose // (2 * experts) * n_high
    share = capacity // n_core
    tokens = tok_rows * n_high
    slots = n_low * capacity
    rows = slots // n_core
    high, low = lax.axis_index("ex"), lax.axis_index("ey")
    swap = [(0, 1), (1, 0)]
    far = n_high // 2
    mid = tok_rows // 2

    def across(x):
        return lax.all_to_all(x, ("tp", "ey"), split_axis=0, concat_axis=0, tiled=True)

    def swapped(x):
        return lax.ppermute(x, "tp", swap)

    def upward(x):
        return lax.ppermute(x, "ex", [(i, (i + 1) % n_high) for i in range(n_high)])

    def downward(x):
        return lax.ppermute(x, "ex", [(i, (i - 1) % n_high) for i in range(n_high)])

    def gathered(x):
        ups, downs = [x], [x]
        for _ in range(far - 1):
            ups.append(upward(ups[-1]))
            downs.append(downward(downs[-1]))
        opposite = [upward(ups[-1][:mid]), downward(downs[-1][mid:])]
        return downs + opposite + ups[:0:-1]

    def scattered(block, beside):
        opposite = block(far)
        up, down = upward(opposite[:mid]), downward(opposite[mid:])
        for i in range(far - 1, 0, -1):
            up, down = lax.optimization_barrier((up, down))
            ahead, behind = block(i), block(n_high - i)
            if i == far - 1:
                ahead = jnp.concatenate(
                    [(ahead[:mid].astype(f32) + up.astype(f32)).astype(bf16), ahead[mid:]], axis=0
                )
                behind = jnp.concatenate(
                    [behind[:mid], (behind[mid:].astype(f32) + down.astype(f32)).astype(bf16)],
                    axis=0,
                )
            else:
                ahead = (ahead.astype(f32) + up.astype(f32)).astype(bf16)
                behind = (behind.astype(f32) + down.astype(f32)).astype(bf16)
            ahead, behind = beside(i, ahead, behind)
            up, down = upward(ahead), downward(behind)
        return up, down

    metas = lax.all_to_all(id_table(expert_ids.T, gate_prob.T, n_high), "ex", 0, 0, tiled=True)
    metas = lax.dynamic_slice_in_dim(jnp.concatenate([metas, metas], axis=0), high, n_high, 0)
    metas = metas[:, :, :tok_rows].astype(f32).transpose(1, 0, 2).reshape(2 * choose, tokens)
    all_ids = metas[:choose].astype(jnp.int32)
    all_probs = metas[choose:]

    mine = lax.broadcasted_iota(jnp.int32, (n_low, 1, 1), 0) + high * n_low
    named = all_ids[None, :, :] == mine
    chosen = jnp.sum(named.astype(f32), axis=1)
    weight = jnp.sum(jnp.where(named, all_probs[None], 0.0), axis=1)
    earlier = (
        lax.broadcasted_iota(jnp.int32, (tokens, tokens), 0)
        < lax.broadcasted_iota(jnp.int32, (tokens, tokens), 1)
    ).astype(bf16)
    rank = dot(chosen.astype(bf16), earlier).astype(jnp.int32)
    rank = jnp.where(chosen > 0, rank, -1)
    place = lax.broadcasted_iota(jnp.int32, (n_core, 1, share, 1), 0) * share
    place = place + lax.broadcasted_iota(jnp.int32, (n_core, 1, share, 1), 2)
    pick = (rank[None, :, None, :] == place).astype(bf16).reshape(slots, tokens)
    pick = lax.optimization_barrier(pick)
    lane = lax.broadcasted_iota(jnp.int32, (1, LANES), 1)
    weights = jnp.concatenate([weight, jnp.zeros((LANES - n_low, tokens), f32)], axis=0)
    weights = weights.T.astype(bf16)

    all_inputs = gathered(layer_input)
    send_inputs = pick_rows(pick, all_inputs, weights)
    gate_own, up_own, down_own = gate_weight[0], up_weight[0], down_weight[0]
    out_grad = after(out_grad, send_inputs)
    in_rows = across(send_inputs)
    gate_other, up_other, down_other = swapped(gate_own), swapped(up_own), swapped(down_own)
    send_grads = pick_rows(pick, gathered(out_grad))
    in_rows, send_grads = lax.optimization_barrier((in_rows, send_grads))
    gr_rows = across(send_grads)

    route_weight = jnp.sum(
        jnp.where(lane == low, in_rows[:rows, half:].astype(f32), 0.0), axis=1, keepdims=True
    )
    in0, in1 = in_rows[:rows, :half], in_rows[rows:, :half]
    forward, acts = [], []
    for gate_w, up_w in ((gate_own, up_own), (gate_other, up_other)):
        gate_pre = dot(in0, gate_w[:half]) + dot(in1, gate_w[half:])
        up_pre = dot(in0, up_w[:half]) + dot(in1, up_w[half:])
        gate_sigmoid = jax.nn.sigmoid(gate_pre)
        silu_gate = gate_pre * gate_sigmoid
        hidden_act = silu_gate * up_pre
        to_gate = route_weight * up_pre * gate_sigmoid * (1.0 + gate_pre * (1.0 - gate_sigmoid))
        to_up = route_weight * silu_gate
        forward += [hidden_act, to_gate, to_up]
        acts.append((route_weight * hidden_act).astype(bf16))
    forward = jnp.stack(forward)
    gr_rows, forward, acts = lax.optimization_barrier((gr_rows, forward, acts))

    mark = jnp.reshape(high * n_low + low, (1,)).astype(jnp.int32)
    back = backward_rows(
        gr_rows,
        forward,
        (down_own, down_other),
        (gate_own, up_own, gate_other, up_other),
        mark,
    )
    other_act, other_rows = swapped(acts[1]), swapped(gr_rows)
    back, other_act, other_rows = lax.optimization_barrier((back, other_act, other_rows))
    home = across(back)

    home, acts, other_act = lax.optimization_barrier((home, acts, other_act))
    opposite = dot(pick[:, far * tok_rows : (far + 1) * tok_rows], home, ((0,), (0,)))
    sums = dot(pick, home, ((0,), (0,))).astype(bf16)
    made, own = [None], [sums[:tok_rows]]

    def beside(i, ahead, behind):
        if i in (1, 2):
            made[0] = outer_sum((acts[0], other_act), (gr_rows, other_rows), 2 - i, made[0])
            ahead, behind, made[0] = lax.optimization_barrier((ahead, behind, made[0]))
        else:
            ahead, behind, own[0] = lax.optimization_barrier((ahead, behind, own[0]))
        return ahead, behind

    def block(i):
        if i == far:
            return opposite.astype(bf16)
        return sums[i * tok_rows : (i + 1) * tok_rows]

    up, down = scattered(block, beside)
    input_grad, prob_grad = last_sum(own[0], up, down, expert_ids)
    return (input_grad, prob_grad.T, made[0][None])


def solution(mesh):
    return jax.shard_map(
        body,
        mesh=mesh,
        in_specs=(
            P(("ex", "ey"), "tp"),
            P(("ex", "ey"), "tp"),
            P(("ex", "ey"), None),
            P(("ex", "ey"), None),
            P(("ex", "ey"), None, "tp"),
            P(("ex", "ey"), None, "tp"),
            P(("ex", "ey"), "tp", None),
        ),
        out_specs=(P(("ex", "ey"), "tp"), P(("ex", "ey"), None), P(("ex", "ey"), "tp", None)),
        check_vma=False,
    )
```

```python
import jax
import jax.numpy as jnp
from jax import lax
from jax.experimental import pallas as pl
from jax.experimental.pallas import tpu as pltpu
from jax.sharding import PartitionSpec as P

LANES = 128
MIB = 1024 * 1024


def dot(a, b, dims=((1,), (0,))):
    return lax.dot_general(a, b, (dims, ((), ())), preferred_element_type=jnp.float32)


def after(x, *earlier):
    return lax.optimization_barrier((x,) + earlier)[0]


def pick_rows(pick, pieces, extra=None):
    slots, tokens = pick.shape
    width = pieces[0].shape[1]
    more = 0 if extra is None else extra.shape[1]
    extras = [] if extra is None else [extra]
    step = 512

    def kernel(pick_ref, *refs):
        piece_refs, extra_refs = refs[: len(pieces)], refs[len(pieces) : len(pieces) + len(extras)]
        out_ref, rows_ref = refs[-2:]
        at = 0
        for ref in piece_refs:
            rows_ref[at : at + ref.shape[0], :] = ref[...]
            at += ref.shape[0]
        for col in range(0, width, step):
            out_ref[:, col : col + step] = dot(
                pick_ref[...], rows_ref[:, col : col + step]
            ).astype(out_ref.dtype)
        for ref in extra_refs:
            out_ref[:, width:] = dot(pick_ref[...], ref[...]).astype(out_ref.dtype)

    return pl.pallas_call(
        kernel,
        out_shape=jax.ShapeDtypeStruct((slots, width + more), jnp.bfloat16),
        scratch_shapes=[pltpu.VMEM((tokens, width), jnp.bfloat16)],
        compiler_params=pltpu.CompilerParams(vmem_limit_bytes=16 * MIB),
        cost_estimate=pl.CostEstimate(
            flops=2 * slots * tokens * (width + more),
            bytes_accessed=2 * (slots + tokens) * (width + more),
            transcendentals=0,
        ),
        name="pick_rows",
    )(pick, *pieces, *extras)


def id_table(ids, probs, copies):
    choose, tokens = ids.shape

    def kernel(ids_hbm, probs_hbm, out_ref, ids_ref, probs_ref, sem):
        ids_copy = pltpu.make_async_copy(ids_hbm, ids_ref, sem.at[0])
        probs_copy = pltpu.make_async_copy(probs_hbm, probs_ref, sem.at[1])
        ids_copy.start()
        probs_copy.start()
        ids_copy.wait()
        probs_copy.wait()
        values = jnp.concatenate(
            [ids_ref[...].astype(jnp.float32), probs_ref[...].astype(jnp.float32)], axis=0
        ).astype(jnp.bfloat16)
        out_ref[...] = jnp.zeros(out_ref.shape, out_ref.dtype)
        for i in range(copies):
            out_ref[i, :, :tokens] = values

    return pl.pallas_call(
        kernel,
        out_shape=jax.ShapeDtypeStruct((copies, 2 * choose, LANES), jnp.bfloat16),
        in_specs=[pl.BlockSpec(memory_space=pl.ANY)] * 2,
        scratch_shapes=[
            pltpu.VMEM(ids.shape, ids.dtype),
            pltpu.VMEM(probs.shape, probs.dtype),
            pltpu.SemaphoreType.DMA((2,)),
        ],
        compiler_params=pltpu.CompilerParams(vmem_limit_bytes=60 * MIB),
        name="id_table",
    )(ids, probs)


def last_sum(sums, up, down, ids):
    tok_rows, width = up.shape
    half = width - LANES
    choose = ids.shape[1]

    def kernel(sums_ref, up_ref, down_ref, ids_ref, grad_ref, prob_ref):
        def total(cols):
            return sum(ref[:, cols].astype(jnp.float32) for ref in (sums_ref, up_ref, down_ref))

        grad_ref[...] = total(slice(0, half)).astype(jnp.bfloat16)
        by_expert = total(slice(half, width))
        lane = lax.broadcasted_iota(jnp.int32, (tok_rows, LANES), 1)
        found = jnp.zeros((tok_rows, LANES), jnp.float32)
        for k in range(choose):
            value = jnp.sum(
                jnp.where(lane == ids_ref[:, k : k + 1], by_expert, 0.0), axis=1, keepdims=True
            )
            found = jnp.where(lane == k, value, found)
        prob_ref[...] = found.T[:choose].astype(jnp.bfloat16)

    def whole(shape):
        return pl.BlockSpec(shape, lambda i: (0, 0))

    return pl.pallas_call(
        kernel,
        grid=(1,),
        out_shape=(
            jax.ShapeDtypeStruct((tok_rows, half), jnp.bfloat16),
            jax.ShapeDtypeStruct((choose, tok_rows), jnp.bfloat16),
        ),
        in_specs=[whole((tok_rows, width))] * 3 + [whole((tok_rows, choose))],
        out_specs=(whole((tok_rows, half)), whole((choose, tok_rows))),
        compiler_params=pltpu.CompilerParams(vmem_limit_bytes=8 * MIB),
        name="last_sum",
    )(sums, up, down, ids)


def backward_rows(gr_rows, forward, downs, ins, mark):
    rows2, half = gr_rows.shape
    rows = rows2 // 2
    hid = downs[0].shape[0]
    width = 2 * half
    chunk = 1024
    tile = 256
    chunks = width // chunk
    n_in = len(ins)

    def kernel(mark_ref, gr_hbm, *refs):
        fwd_hbm, refs = refs[0], refs[1:]
        down_hbm, refs = refs[:2], refs[2:]
        in_hbm, refs = refs[:n_in], refs[n_in:]
        out_hbm, gr_ref, down_ref, fwd_ref, in_ref, grads_ref, out_ref, *refs = refs
        gr_sem, down_sem, fwd_sem, in_sem, out_sem = refs
        fwd_copy = pltpu.make_async_copy(fwd_hbm, fwd_ref, fwd_sem)
        gr_copies, down_copies, in_copies = [], [], []
        spans = []
        for h in range(2):
            for col in range(0, half, chunk):
                n = len(spans)
                spans.append((h, col))
                span = (pl.ds(h * rows, rows), pl.ds(col, chunk))
                gr_copies.append(
                    pltpu.make_async_copy(gr_hbm.at[span], gr_ref.at[span], gr_sem.at[n])
                )
                cols = pl.ds(h * half + col, chunk)
                for w in range(2):
                    down_copies.append(
                        pltpu.make_async_copy(
                            down_hbm[w].at[:, cols],
                            down_ref.at[pl.ds(w * hid, hid), cols],
                            down_sem.at[2 * n + w],
                        )
                    )
        for c in range(chunks):
            at = pl.ds(c * chunk, chunk)
            for w in range(n_in):
                in_copies.append(
                    pltpu.make_async_copy(
                        in_hbm[w].at[at],
                        in_ref.at[at, pl.ds(w * hid, hid)],
                        in_sem.at[c * n_in + w],
                    )
                )
        for n in range(len(spans)):
            gr_copies[n].start()
            down_copies[2 * n].start()
            down_copies[2 * n + 1].start()
        fwd_copy.start()

        last = ((1,), (1,))
        total = None
        for n, (h, col) in enumerate(spans):
            gr_copies[n].wait()
            down_copies[2 * n].wait()
            down_copies[2 * n + 1].wait()
            part = dot(
                gr_ref[h * rows : (h + 1) * rows, col : col + chunk],
                down_ref[:, h * half + col : h * half + col + chunk],
                last,
            )
            for copy in in_copies[n * n_in : (n + 1) * n_in]:
                copy.start()
            total = part if total is None else total + part
        fwd_copy.wait()
        prob = jnp.zeros((rows, 1), jnp.float32)
        for w in range(2):
            act, to_gate, to_up = (fwd_ref[i] for i in range(3 * w, 3 * w + 3))
            hidden_grad = total[:, w * hid : (w + 1) * hid]
            prob = prob + jnp.sum(hidden_grad * act, axis=1, keepdims=True)
            at = 2 * w * hid
            grads_ref[:, at : at + hid] = (hidden_grad * to_gate).astype(jnp.bfloat16)
            grads_ref[:, at + hid : at + 2 * hid] = (hidden_grad * to_up).astype(jnp.bfloat16)
        lane = lax.broadcasted_iota(jnp.int32, (rows, LANES), 1)
        marked = jnp.where(lane == mark_ref[0], prob, 0.0).astype(jnp.bfloat16)
        out_copies = []

        def send(h, first, size):
            span = (pl.ds(h * rows, rows), pl.ds(first, size))
            out_copies.append(
                pltpu.make_async_copy(
                    out_ref.at[span], out_hbm.at[span], out_sem.at[len(out_copies)]
                )
            )
            out_copies[-1].start()

        for h in range(2):
            out_ref[h * rows : (h + 1) * rows, half:] = marked
            send(h, half, LANES)
        for c in range(chunks):
            for copy in in_copies[c * n_in : (c + 1) * n_in]:
                copy.wait()
            h, first = divmod(c * chunk, half)
            for col in range(0, chunk, tile):
                weights = in_ref[c * chunk + col : c * chunk + col + tile, :]
                out_ref[h * rows : (h + 1) * rows, first + col : first + col + tile] = dot(
                    grads_ref[...], weights, last
                ).astype(jnp.bfloat16)
            send(h, first, chunk)
        for copy in out_copies:
            copy.wait()

    hbm = pl.BlockSpec(memory_space=pltpu.HBM)
    return pl.pallas_call(
        kernel,
        out_shape=jax.ShapeDtypeStruct((rows2, half + LANES), jnp.bfloat16),
        in_specs=[
            pl.BlockSpec(memory_space=pltpu.SMEM),
            pl.BlockSpec(memory_space=pl.ANY),
        ]
        + [hbm] * (3 + n_in),
        out_specs=hbm,
        scratch_shapes=[
            pltpu.VMEM((rows2, half), jnp.bfloat16),
            pltpu.VMEM((2 * hid, width), jnp.bfloat16),
            pltpu.VMEM((6, rows, hid), jnp.float32),
            pltpu.VMEM((width, n_in * hid), jnp.bfloat16),
            pltpu.VMEM((rows, n_in * hid), jnp.bfloat16),
            pltpu.VMEM((rows2, half + LANES), jnp.bfloat16),
            pltpu.SemaphoreType.DMA((chunks,)),
            pltpu.SemaphoreType.DMA((2 * chunks,)),
            pltpu.SemaphoreType.DMA,
            pltpu.SemaphoreType.DMA((chunks * n_in,)),
            pltpu.SemaphoreType.DMA((chunks + 2,)),
        ],
        compiler_params=pltpu.CompilerParams(vmem_limit_bytes=50 * MIB),
        cost_estimate=pl.CostEstimate(
            flops=2 * rows * width * 6 * hid,
            bytes_accessed=2 * width * 6 * hid + 8 * rows2 * half,
            transcendentals=0,
        ),
        name="backward_rows",
    )(mark, gr_rows, forward, *downs, *ins)


def outer_sum(acts, grads, h, into=None):
    rows, hid = acts[0].shape
    half = grads[0].shape[1]
    step = 512
    n = len(acts)
    old = [] if into is None else [into]

    def kernel(*refs):
        act_refs, gr_refs = refs[:n], refs[n : 2 * n]
        out_hbm, out_ref, sem = refs[-3:]
        copies = []
        for i, col in enumerate(range(0, half, step)):
            value = sum(
                dot(a[...], g[:, col : col + step], ((0,), (0,)))
                for a, g in zip(act_refs, gr_refs)
            )
            out_ref[:, col : col + step] = value.astype(jnp.bfloat16)
            copies.append(
                pltpu.make_async_copy(
                    out_ref.at[:, pl.ds(col, step)],
                    out_hbm.at[:, pl.ds(h * half + col, step)],
                    sem.at[i],
                )
            )
            copies[-1].start()
        for copy in copies:
            copy.wait()

    return pl.pallas_call(
        kernel,
        out_shape=jax.ShapeDtypeStruct((hid, 2 * half), jnp.bfloat16),
        grid=(1,),
        in_specs=[pl.BlockSpec((rows, hid), lambda i: (0, 0))] * n
        + [pl.BlockSpec((rows, half), lambda i: (h, 0))] * n
        + [pl.BlockSpec(memory_space=pltpu.HBM)] * len(old),
        out_specs=pl.BlockSpec(memory_space=pltpu.HBM),
        scratch_shapes=[
            pltpu.VMEM((hid, half), jnp.bfloat16),
            pltpu.SemaphoreType.DMA((half // step,)),
        ],
        input_output_aliases={2 * n: 0} if old else {},
        compiler_params=pltpu.CompilerParams(vmem_limit_bytes=24 * MIB),
        cost_estimate=pl.CostEstimate(
            flops=4 * rows * half * hid, bytes_accessed=6 * hid * half, transcendentals=0
        ),
        name="outer_sum",
    )(*acts, *grads, *old)


def body(layer_input, out_grad, gate_prob, expert_ids, gate_weight, up_weight, down_weight):
    bf16, f32 = jnp.bfloat16, jnp.float32
    tok_rows, choose = expert_ids.shape
    half = layer_input.shape[1]
    n_high, n_low, n_core = lax.axis_size("ex"), lax.axis_size("ey"), lax.axis_size("tp")
    experts = n_high * n_low
    capacity = 3 * tok_rows * choose // (2 * experts) * n_high
    share = capacity // n_core
    tokens = tok_rows * n_high
    slots = n_low * capacity
    rows = slots // n_core
    high, low = lax.axis_index("ex"), lax.axis_index("ey")
    swap = [(0, 1), (1, 0)]
    far = n_high // 2
    mid = tok_rows // 2

    def across(x):
        return lax.all_to_all(x, ("tp", "ey"), split_axis=0, concat_axis=0, tiled=True)

    def swapped(x):
        return lax.ppermute(x, "tp", swap)

    def upward(x):
        return lax.ppermute(x, "ex", [(i, (i + 1) % n_high) for i in range(n_high)])

    def downward(x):
        return lax.ppermute(x, "ex", [(i, (i - 1) % n_high) for i in range(n_high)])

    def gathered(x):
        ups, downs = [x], [x]
        for _ in range(far - 1):
            ups.append(upward(ups[-1]))
            downs.append(downward(downs[-1]))
        opposite = [upward(ups[-1][:mid]), downward(downs[-1][mid:])]
        return downs + opposite + ups[:0:-1]

    def scattered(block, beside):
        opposite = block(far)
        up, down = upward(opposite[:mid]), downward(opposite[mid:])
        for i in range(far - 1, 0, -1):
            up, down = lax.optimization_barrier((up, down))
            ahead, behind = block(i), block(n_high - i)
            if i == far - 1:
                ahead = jnp.concatenate(
                    [(ahead[:mid].astype(f32) + up.astype(f32)).astype(bf16), ahead[mid:]], axis=0
                )
                behind = jnp.concatenate(
                    [behind[:mid], (behind[mid:].astype(f32) + down.astype(f32)).astype(bf16)],
                    axis=0,
                )
            else:
                ahead = (ahead.astype(f32) + up.astype(f32)).astype(bf16)
                behind = (behind.astype(f32) + down.astype(f32)).astype(bf16)
            ahead, behind = beside(i, ahead, behind)
            up, down = upward(ahead), downward(behind)
        return up, down

    metas = lax.all_to_all(id_table(expert_ids.T, gate_prob.T, n_high), "ex", 0, 0, tiled=True)
    metas = lax.dynamic_slice_in_dim(jnp.concatenate([metas, metas], axis=0), high, n_high, 0)
    metas = metas[:, :, :tok_rows].astype(f32).transpose(1, 0, 2).reshape(2 * choose, tokens)
    all_ids = metas[:choose].astype(jnp.int32)
    all_probs = metas[choose:]

    mine = lax.broadcasted_iota(jnp.int32, (n_low, 1, 1), 0) + high * n_low
    named = all_ids[None, :, :] == mine
    chosen = jnp.sum(named.astype(f32), axis=1)
    weight = jnp.sum(jnp.where(named, all_probs[None], 0.0), axis=1)
    earlier = (
        lax.broadcasted_iota(jnp.int32, (tokens, tokens), 0)
        < lax.broadcasted_iota(jnp.int32, (tokens, tokens), 1)
    ).astype(bf16)
    rank = dot(chosen.astype(bf16), earlier).astype(jnp.int32)
    rank = jnp.where(chosen > 0, rank, -1)
    place = lax.broadcasted_iota(jnp.int32, (n_core, 1, share, 1), 0) * share
    place = place + lax.broadcasted_iota(jnp.int32, (n_core, 1, share, 1), 2)
    pick = (rank[None, :, None, :] == place).astype(bf16).reshape(slots, tokens)
    pick = lax.optimization_barrier(pick)
    lane = lax.broadcasted_iota(jnp.int32, (1, LANES), 1)
    weights = jnp.concatenate([weight, jnp.zeros((LANES - n_low, tokens), f32)], axis=0)
    weights = weights.T.astype(bf16)

    all_inputs = gathered(layer_input)
    send_inputs = pick_rows(pick, all_inputs, weights)
    gate_own, up_own, down_own = gate_weight[0], up_weight[0], down_weight[0]
    out_grad = after(out_grad, send_inputs)
    in_rows = across(send_inputs)
    gate_other, up_other, down_other = swapped(gate_own), swapped(up_own), swapped(down_own)
    send_grads = pick_rows(pick, gathered(out_grad))
    in_rows, send_grads = lax.optimization_barrier((in_rows, send_grads))
    gr_rows = across(send_grads)

    route_weight = jnp.sum(
        jnp.where(lane == low, in_rows[:rows, half:].astype(f32), 0.0), axis=1, keepdims=True
    )
    in0, in1 = in_rows[:rows, :half], in_rows[rows:, :half]
    forward, acts = [], []
    for gate_w, up_w in ((gate_own, up_own), (gate_other, up_other)):
        gate_pre = dot(in0, gate_w[:half]) + dot(in1, gate_w[half:])
        up_pre = dot(in0, up_w[:half]) + dot(in1, up_w[half:])
        gate_sigmoid = jax.nn.sigmoid(gate_pre)
        silu_gate = gate_pre * gate_sigmoid
        hidden_act = silu_gate * up_pre
        to_gate = route_weight * up_pre * gate_sigmoid * (1.0 + gate_pre * (1.0 - gate_sigmoid))
        to_up = route_weight * silu_gate
        forward += [hidden_act, to_gate, to_up]
        acts.append((route_weight * hidden_act).astype(bf16))
    forward = jnp.stack(forward)
    gr_rows, forward, acts = lax.optimization_barrier((gr_rows, forward, acts))

    mark = jnp.reshape(high * n_low + low, (1,)).astype(jnp.int32)
    back = backward_rows(
        gr_rows,
        forward,
        (down_own, down_other),
        (gate_own, up_own, gate_other, up_other),
        mark,
    )
    other_act, other_rows = swapped(acts[1]), swapped(gr_rows)
    back, other_act, other_rows = lax.optimization_barrier((back, other_act, other_rows))
    home = across(back)

    home, acts, other_act = lax.optimization_barrier((home, acts, other_act))
    opposite = dot(pick[:, far * tok_rows : (far + 1) * tok_rows], home, ((0,), (0,)))
    opposite = opposite.astype(bf16)
    home, opposite = lax.optimization_barrier((home, opposite))
    sums = dot(pick, home, ((0,), (0,))).astype(bf16)
    made, own = [None], [sums[:tok_rows]]

    def beside(i, ahead, behind):
        if i in (1, 2):
            made[0] = outer_sum((acts[0], other_act), (gr_rows, other_rows), 2 - i, made[0])
            ahead, behind, made[0] = lax.optimization_barrier((ahead, behind, made[0]))
        else:
            ahead, behind, own[0] = lax.optimization_barrier((ahead, behind, own[0]))
        return ahead, behind

    def block(i):
        if i == far:
            return opposite
        return sums[i * tok_rows : (i + 1) * tok_rows]

    up, down = scattered(block, beside)
    input_grad, prob_grad = last_sum(own[0], up, down, expert_ids)
    return (input_grad, prob_grad.T, made[0][None])


def solution(mesh):
    return jax.shard_map(
        body,
        mesh=mesh,
        in_specs=(
            P(("ex", "ey"), "tp"),
            P(("ex", "ey"), "tp"),
            P(("ex", "ey"), None),
            P(("ex", "ey"), None),
            P(("ex", "ey"), None, "tp"),
            P(("ex", "ey"), None, "tp"),
            P(("ex", "ey"), "tp", None),
        ),
        out_specs=(P(("ex", "ey"), "tp"), P(("ex", "ey"), None), P(("ex", "ey"), "tp", None)),
        check_vma=False,
    )
```
